128 devices in a mesh: gx: 32 (over z, x, core), gz: 4 (over y).
Axes of the slice: x: 4, y: 4, z: 4, core: 2. Of those that a mesh axis runs over, the one named last changes fastest.
Arguments:
- thermal_state: float32 [256, 64, 512], P('gx', None, 'gz'), may hold values from -6 to 6
- heat_spread_factor: float32 [256, 64, 512], P('gx', None, 'gz'), may hold values from 0.25 to 2
- heating_input: float32 [256, 64, 512], P('gx', None, 'gz'), may hold values from -400 to 400
Outputs:
- next_temperature: float32 [256, 64, 512], P('gx', None, 'gz')
The draws below stay inside these ranges and needn't reach their ends.
All inputs are finite; a program needn't handle non-finite values.
Results may differ from the reference program's by a relative error of at most 0.0003.
Values sent between devices are 32-bit elements; how exact they have to be, the bound alone decides.
No kernel may reach another device: no remote copies, remote signals or barrier semaphores. Data moves between devices by JAX's collectives and lax.ppermute only.
A program may use at most 64 MiB of HBM per device.

```python
import math
import jax
import jax.numpy as jnp
from jax import lax

SHARD_SPAN_WIDTH = 8
VOLUMES_BY_ROW = 64
SHARD_SPAN_TALL = 128
TOTAL_SPAN_WIDTH = 256
TOTAL_SPAN_TALL = 512


def draw_heating_input(key, part):
    return jnp.clip(100.0 * jax.random.normal(key, (TOTAL_SPAN_WIDTH, VOLUMES_BY_ROW, TOTAL_SPAN_TALL), jnp.float32), -400.0, 400.0)


def steps_of(rng, shape, pieces, low, top_value):
    gain, own = 1.0, jax.random.fold_in(rng, 6)
    for axis_at, blocks in pieces:
        heights = jnp.exp(jax.random.uniform(jax.random.fold_in(own, axis_at), (blocks,), jnp.float32, low / len(pieces), top_value / len(pieces)))
        gain = gain * jnp.repeat(heights, shape[axis_at] // blocks).reshape([-1 if axis == axis_at else 1 for axis in range(len(shape))])
    return gain


def normal_values(key, shape, scale, reach, shards=(), kind=jnp.bfloat16):
    level = steps_of(key, shape, shards, -0.22, 0.18) if shards else 1.0
    array = jax.random.normal(key, shape, jnp.float32) * scale * level
    return jnp.minimum(jnp.maximum(array, -reach), reach).astype(kind)


def setup_inputs(seed: int = 0) -> dict:
    key_of = jax.random.split(jax.random.key(seed), 4)
    return {
        "thermal_state": normal_values(key_of[0], (TOTAL_SPAN_WIDTH, VOLUMES_BY_ROW, TOTAL_SPAN_TALL), 1.0, 6.0, ((0, 32), (2, 4)), jnp.float32),
        "heat_spread_factor": jnp.clip(jnp.exp(math.log(2.0) - 2.0794415 * jax.random.uniform(key_of[1], (TOTAL_SPAN_WIDTH, VOLUMES_BY_ROW, TOTAL_SPAN_TALL), jnp.float32) ** steps_of(key_of[1], (TOTAL_SPAN_WIDTH, VOLUMES_BY_ROW, TOTAL_SPAN_TALL), ((0, 32), (2, 4)), -0.2, 0.2)), 0.25, 2.0),
        "heating_input": draw_heating_input(jax.random.fold_in(key_of[3], 71), 0),
    }


half_theta = 0.5


def cut_range(values, start, stop, direction):
    return lax.slice_in_dim(values, start, stop, axis=direction % values.ndim)


def from_below(values, stride, direction):
    position = direction % values.ndim
    extent = values.shape[position]
    if stride >= extent:
        return jnp.zeros_like(values)
    retained = cut_range(values, 0, extent - stride, direction)
    padding = jnp.zeros_like(cut_range(values, 0, stride, direction))
    return jnp.concatenate([padding, retained], axis=position)


def from_above(values, stride, direction):
    position = direction % values.ndim
    extent = values.shape[position]
    if stride >= extent:
        return jnp.zeros_like(values)
    retained = cut_range(values, stride, extent, direction)
    padding = jnp.zeros_like(cut_range(values, 0, stride, direction))
    return jnp.concatenate([retained, padding], axis=position)


def eliminate(lower_band, upper_band, values, low_lower, low_upper, low_values, high_lower, high_upper, high_values):
    denominator = 1.0 - lower_band * low_upper - upper_band * high_lower
    new_lower = -lower_band * low_lower
    new_upper = -upper_band * high_upper
    new_values = values - lower_band * low_values - upper_band * high_values
    return new_lower / denominator, new_upper / denominator, new_values / denominator


def reduce_levels(lower_band, upper_band, values, direction):
    extent = lower_band.shape[direction % lower_band.ndim]
    stride = 1
    while stride < extent:
        lower_band, upper_band, values = eliminate(
            lower_band, upper_band, values,
            from_below(lower_band, stride, direction), from_below(upper_band, stride, direction),
            from_below(values, stride, direction),
            from_above(lower_band, stride, direction), from_above(upper_band, stride, direction),
            from_above(values, stride, direction))
        stride = stride * 2
    return values


def axis_flux_parts(temp_pad, cond_pad, ratio, direction):
    extent = temp_pad.shape[direction] - 2
    face_all = 0.5 * (cut_range(cond_pad, 0, extent + 1, direction) + cut_range(cond_pad, 1, extent + 2, direction))
    face_low = cut_range(face_all, 0, extent, direction)
    face_high = cut_range(face_all, 1, extent + 1, direction)
    centre = cut_range(temp_pad, 1, extent + 1, direction)
    lower_cell = cut_range(temp_pad, 0, extent, direction)
    upper_cell = cut_range(temp_pad, 2, extent + 2, direction)
    explicit = ratio * (face_high * (upper_cell - centre) - face_low * (centre - lower_cell))
    lower_band = (-half_theta * ratio) * face_low
    upper_band = (-half_theta * ratio) * face_high
    main_band = 1.0 - lower_band - upper_band
    return explicit, lower_band, main_band, upper_band


def reference(thermal_state, heat_spread_factor, heating_input):
    width_with_ghosts = [(1, 1), (0, 0), (0, 0)]
    row_with_ghosts = [(0, 0), (1, 1), (0, 0)]
    height_with_ghosts = [(0, 0), (0, 0), (1, 1)]
    width_known_flux, width_subdiagonal, width_diagonal, width_superdiagonal = axis_flux_parts(jnp.pad(thermal_state, width_with_ghosts), jnp.pad(heat_spread_factor, width_with_ghosts), 16.0 * SHARD_SPAN_WIDTH * SHARD_SPAN_WIDTH, 0)
    row_known_flux, row_subdiagonal, row_diagonal, row_superdiagonal = axis_flux_parts(jnp.pad(thermal_state, row_with_ghosts), jnp.pad(heat_spread_factor, row_with_ghosts), 2.0, 1)
    height_known_flux, height_subdiagonal, height_diagonal, height_superdiagonal = axis_flux_parts(jnp.pad(thermal_state, height_with_ghosts), jnp.pad(heat_spread_factor, height_with_ghosts), 0.5 * SHARD_SPAN_TALL * SHARD_SPAN_TALL, 2)
    right_side = ((width_known_flux + row_known_flux) + height_known_flux) + heating_input
    step_one = reduce_levels(width_subdiagonal / width_diagonal, width_superdiagonal / width_diagonal, right_side / width_diagonal, 0)
    step_two = reduce_levels(row_subdiagonal / row_diagonal, row_superdiagonal / row_diagonal, step_one / row_diagonal, 1)
    closing_update = reduce_levels(height_subdiagonal / height_diagonal, height_superdiagonal / height_diagonal, step_two / height_diagonal, 2)
    return thermal_state + closing_update
```

```python
import functools

import jax
import jax.numpy as jnp
from jax import lax
from jax.experimental import pallas as pl
from jax.experimental.pallas import tpu as pltpu
from jax.sharding import PartitionSpec as P

NX, NY, NZ = 8, 64, 128
ROWS = NX * NY
HALF = NY // 2
CX = 0.25 * 16.0 * NX * NX
CY = 0.25 * 2.0
CZ = 0.25 * 0.5 * NZ * NZ
F32 = jnp.float32
VMEM_LIMIT = 24 * 1024 * 1024
HIGHEST = lax.Precision.HIGHEST


def call(kernel, outs, *args, scratch=(), flops=0, name=None):
    shapes = [jax.ShapeDtypeStruct(s, F32) for s in outs]
    nbytes = sum(4 * a.size for a in args) + sum(4 * s.size for s in shapes)
    return pl.pallas_call(
        kernel,
        out_shape=shapes,
        in_specs=[pl.BlockSpec(memory_space=pltpu.VMEM) for _ in args],
        out_specs=[pl.BlockSpec(memory_space=pltpu.VMEM) for _ in outs],
        scratch_shapes=[pltpu.VMEM(s, F32) for s in scratch],
        compiler_params=pltpu.CompilerParams(vmem_limit_bytes=VMEM_LIMIT),
        cost_estimate=pl.CostEstimate(flops=flops, bytes_accessed=nbytes, transcendentals=0),
        name=name,
    )(*args)


def lanes_to_rows(select, block):
    return lax.dot_general(
        select, block, (((1,), (1,)), ((), ())), precision=HIGHEST, preferred_element_type=F32
    )


def rows_to_lanes(rows, select):
    return lax.dot_general(
        rows, select, (((0,), (0,)), ((), ())), precision=HIGHEST, preferred_element_type=F32
    )


def selector(entries):
    row = lax.broadcasted_iota(jnp.int32, (8, NZ), 0)
    lane = lax.broadcasted_iota(jnp.int32, (8, NZ), 1)
    hit = None
    for r, l in entries:
        one = (row == r) if l is None else ((row == r) & (lane == l))
        hit = one if hit is None else (hit | one)
    return jnp.where(hit, 1.0, 0.0).astype(F32)


def reduce_chain(e, c, r):
    n = len(e)
    e_h, r_h = e[0], r[0]
    s, w, rr = e[1], c[0], r[1]
    parts = []
    for j in range(1, n - 1):
        inv = 1.0 / (s + w + c[j])
        a, m = w * inv, c[j] * inv
        parts.append((a, m, rr * inv))
        e_h = e_h + a * s
        r_h = r_h + a * rr
        s = e[j + 1] + m * s
        rr = r[j + 1] + m * rr
        w = m * w
    return (e_h, s, w, r_h, rr), parts


def expand_chain(first, last, parts):
    values = [last]
    for a, m, q in reversed(parts):
        values.append(q + a * first + m * values[-1])
    values.append(first)
    return values[::-1]


def solve_chain(e, c, r):
    n = len(e)
    s, rr = e[0], r[0]
    parts = []
    for j in range(n - 1):
        inv = 1.0 / (s + c[j])
        m = c[j] * inv
        parts.append((m, rr * inv))
        s = e[j + 1] + m * s
        rr = r[j + 1] + m * rr
    values = [rr / s]
    for m, q in reversed(parts):
        values.append(q + m * values[-1])
    return values[::-1]


def chain_of(blocks, scale):
    e, c, r = [], [], []
    for i, b in enumerate(blocks):
        e += [b[0], b[1]]
        r += [b[3], b[4]]
        c.append(b[2])
        if i + 1 < len(blocks):
            c.append(scale * (b[6] + blocks[i + 1][5]))
    return e, c, r


def edges_kernel(u_ref, k_ref, out_ref):
    u = u_ref[...].reshape(ROWS, NZ)
    k = k_ref[...].reshape(ROWS, NZ)
    out_ref[...] = lanes_to_rows(selector([(0, 0), (1, NZ - 1)]), u) + lanes_to_rows(
        selector([(2, 0), (3, NZ - 1)]), k
    )


def local_kernel(u_ref, k_ref, f_ref, rp_ref, a_ref, m_ref, inv_ref, ew_ref):
    row = lax.broadcasted_iota(jnp.int32, (NY, NZ), 0)
    lane = lax.broadcasted_iota(jnp.int32, (NY, NZ), 1)
    for x in range(NX):
        u, k = u_ref[x], k_ref[x]
        flux_y = (CY * (k + pltpu.roll(k, NY - 1, 0))) * (pltpu.roll(u, NY - 1, 0) - u)
        flux_y = jnp.where(row == NY - 1, -(CY * k) * u, flux_y)
        low_y = jnp.where(row == 0, (CY * k) * u, pltpu.roll(flux_y, 1, 0))
        flux_z = (CZ * (k + pltpu.roll(k, NZ - 1, 1))) * (pltpu.roll(u, NZ - 1, 1) - u)
        flux_z = jnp.where(lane == NZ - 1, 0.0, flux_z)
        low_z = pltpu.roll(flux_z, 1, 1)
        rp_ref[x] = u + (flux_y - low_y) + (flux_z - low_z) + 0.5 * f_ref[x]
    s = jnp.ones((NY, NZ), F32)
    e_h = s
    w = CX * (k_ref[0] + k_ref[1])
    for j in range(1, NX - 1):
        c = CX * (k_ref[j] + k_ref[j + 1])
        inv = 1.0 / (s + w + c)
        a, m = w * inv, c * inv
        inv_ref[j - 1], a_ref[j - 1], m_ref[j - 1] = inv, a, m
        e_h = e_h + a * s
        s = 1.0 + m * s
        w = m * w
    ew_ref[0], ew_ref[1], ew_ref[2] = e_h, s, w


def halo_kernel(own_ref, one_ref, two_ref, rp_ref, a_ref, m_ref, ew_ref, k_ref, keep_ref, send_ref, rr_ref, fix_ref):
    g = lax.axis_index("gz")
    core = lax.rem(lax.axis_index("gx"), 2)
    odd = lax.rem(g, 2) == 1
    own, one, two = own_ref[...], one_ref[...], two_ref[...]
    low = jnp.where(odd, one, two) * jnp.where(g > 0, 1.0, 0.0)
    high = jnp.where(odd, two, one) * jnp.where(g < 3, 1.0, 0.0)
    at_low = CZ * (low[3:4] + own[2:3]) * (low[1:2] - own[0:1])
    at_high = CZ * (high[2:3] + own[3:4]) * (high[0:1] - own[1:2])
    row = lax.broadcasted_iota(jnp.int32, (8, ROWS), 0)
    both = jnp.where(row == 0, at_low, jnp.where(row == 1, at_high, 0.0))
    fix_ref[...] = rows_to_lanes(both, selector([(0, 0), (1, NZ - 1)])).reshape(NX, NY, NZ)
    for which, out in ((core, keep_ref), (1 - core, send_ref)):
        ys = pl.ds(pl.multiple_of(which * HALF, HALF), HALF)
        r_h = rp_ref[0, ys] + fix_ref[0, ys]
        rr = rp_ref[1, ys] + fix_ref[1, ys]
        for j in range(1, NX - 1):
            rr_ref[j - 1, ys] = rr
            r_h = r_h + a_ref[j - 1, ys] * rr
            rr = (rp_ref[j + 1, ys] + fix_ref[j + 1, ys]) + m_ref[j - 1, ys] * rr
        for i in range(3):
            out[i] = ew_ref[i, ys]
        out[3], out[4] = r_h, rr
        out[5], out[6] = k_ref[0, ys], k_ref[NX - 1, ys]


def core_kernel(own_ref, got_ref, out_ref, parts_ref):
    first = lax.rem(lax.axis_index("gx"), 2) == 0
    low = [jnp.where(first, own_ref[i], got_ref[i]) for i in range(7)]
    high = [jnp.where(first, got_ref[i], own_ref[i]) for i in range(7)]
    port, parts = reduce_chain(*chain_of([low, high], CX))
    for i, v in enumerate(port):
        out_ref[i] = v
    out_ref[5], out_ref[6] = low[5], high[6]
    for j, p in enumerate(parts):
        for i in range(3):
            parts_ref[3 * j + i] = p[i]


def ordered(me, refs, held):
    for i, ref in enumerate(refs):
        held[jnp.bitwise_xor(me, i)] = ref[...]
    return held


def chips_kernel(own_ref, one_ref, two_ref, three_ref, out_ref, parts_ref, held):
    me = lax.rem(lax.axis_index("gx") // 2, 4)
    ordered(me, (own_ref, one_ref, two_ref, three_ref), held)
    blocks = [[held[b, i] for i in range(7)] for b in range(4)]
    port, parts = reduce_chain(*chain_of(blocks, CX))
    for i, v in enumerate(port):
        out_ref[i] = v
    out_ref[5], out_ref[6] = blocks[0][5], blocks[3][6]
    for j, p in enumerate(parts):
        for i in range(3):
            parts_ref[3 * j + i] = p[i]


def back_kernel(own_ref, one_ref, two_ref, three_ref, chips_ref, cores_ref, keep_ref, send_ref, held, nodes):
    index = lax.axis_index("gx")
    core, x, z = lax.rem(index, 2), lax.rem(index // 2, 4), index // 8
    ordered(z, (own_ref, one_ref, two_ref, three_ref), held)
    blocks = [[held[b, i] for i in range(7)] for b in range(4)]
    e, c, r = chain_of(blocks, CX)
    e[0] = e[0] + CX * blocks[0][5]
    e[-1] = e[-1] + CX * blocks[3][6]
    for i, v in enumerate(solve_chain(e, c, r)):
        nodes[i] = v
    first, last = nodes[2 * z], nodes[2 * z + 1]
    parts = [tuple(chips_ref[3 * j + i] for i in range(3)) for j in range(6)]
    for i, v in enumerate(expand_chain(first, last, parts)):
        nodes[i] = v
    first, last = nodes[2 * x], nodes[2 * x + 1]
    parts = [tuple(cores_ref[3 * j + i] for i in range(3)) for j in range(2)]
    v = expand_chain(first, last, parts)
    even = core == 0
    keep_ref[0], keep_ref[1] = jnp.where(even, v[0], v[2]), jnp.where(even, v[1], v[3])
    send_ref[0], send_ref[1] = jnp.where(even, v[2], v[0]), jnp.where(even, v[3], v[1])


def prepare_kernel(u_ref, k_ref, a_ref, m_ref, inv_ref, rr_ref, base_ref, g_ref, h_ref, my_ref, iy_ref):
    base_ref[0] = -u_ref[0]
    base_ref[NX - 1] = -u_ref[NX - 1]
    y = jnp.zeros((NY, NZ), F32)
    g = y
    h = jnp.ones((NY, NZ), F32)
    for j in range(NX - 2, 0, -1):
        m = m_ref[j - 1]
        y = rr_ref[j - 1] * inv_ref[j - 1] + m * y
        g = a_ref[j - 1] + m * g
        h = m * h
        base_ref[j], g_ref[j - 1], h_ref[j - 1] = y - u_ref[j], g, h
    k2 = k_ref.reshape(ROWS, NZ)
    at = lambda y: k2[pl.ds(y, NX, stride=NY), :]
    mid = HALF
    ends = []
    for start, step in ((0, 1), (NY - 1, -1)):
        k = at(start)
        ends.append([1.0 + CY * k, k, start, step])
    while any(e[2] != mid for e in ends):
        for e in ends:
            s, k, y, step = e
            if y == mid:
                continue
            k_next = at(y + step)
            c = CY * (k + k_next)
            inv = 1.0 / (s + c)
            m = c * inv
            my_ref[y], iy_ref[y] = m, inv
            e[0] = (0.0 if y + step == mid else 1.0) + m * s
            e[1], e[2] = k_next, y + step
    iy_ref[mid] = 1.0 / (1.0 + ends[0][0] + ends[1][0])
    my_ref[mid] = jnp.zeros((NX, NZ), F32)


def z_levels(k, r):
    lane = lax.broadcasted_iota(jnp.int32, k.shape, 1)
    up = CZ * (k + pltpu.roll(k, NZ - 1, 1))
    low = pltpu.roll(up, 1, 1)
    top = up
    e = jnp.ones(k.shape, F32)
    s = 1
    while s < NZ:
        inv = 1.0 / (e + low + up)
        has_low, has_up = lane >= s + 1, lane <= NZ - 2 - s
        share = e * inv
        low_in, up_in = jnp.where(has_low, low, 0.0), jnp.where(has_up, up, 0.0)
        e = e + low_in * pltpu.roll(share, s, 1) + up_in * pltpu.roll(share, NZ - s, 1)
        if r is not None:
            q = r * inv
            r = r + low_in * pltpu.roll(q, s, 1) + up_in * pltpu.roll(q, NZ - s, 1)
        new_low = jnp.where(has_low, low * pltpu.roll(low * inv, s, 1), low)
        up = jnp.where(has_up, up * pltpu.roll(up * inv, NZ - s, 1), up)
        low = new_low
        s *= 2
    inv = 1.0 / (e + low + up)
    first, last = lane == 0, lane == NZ - 1
    if r is not None:
        return jnp.where(first | last, 0.0, r * inv)
    g = jnp.where(first, 1.0, jnp.where(last, 0.0, low * inv))
    h = jnp.where(first, 0.0, jnp.where(last, 1.0, up * inv))
    return g, h, jnp.where(lane == NZ - 2, top * g, 0.0)


STEP = 32


def z_ports_kernel(k_ref, after_ref, g_ref, h_ref, port_ref, t_ref):
    del after_ref
    k2 = k_ref.reshape(ROWS, NZ)
    g2, h2 = g_ref.reshape(ROWS, NZ), h_ref.reshape(ROWS, NZ)

    def body(i, carry):
        y = i * STEP
        k = jnp.concatenate([k2[pl.ds(y + n, NX, stride=NY), :] for n in range(STEP)], axis=0)
        g, h, w = z_levels(k, None)
        at = pl.ds(pl.multiple_of(y * NX, NX * STEP), NX * STEP)
        g2[at, :], h2[at, :] = g, h
        t_ref[0, at, :], t_ref[1, at, :] = k, w
        return carry

    lax.fori_loop(0, NY // STEP, body, 0)
    port_ref[...] = (
        lanes_to_rows(selector([(0, None)]), g2[...])
        + lanes_to_rows(selector([(1, None)]), h2[...])
        + lanes_to_rows(selector([(2, None)]), t_ref[1])
        + lanes_to_rows(selector([(5, 0), (6, NZ - 1)]), t_ref[0])
    )


def y_kernel(keep_ref, got_ref, base_ref, gx_ref, hx_ref, my_ref, iy_ref, g_ref, h_ref, port_ref, v_ref, out_ref, b_ref, s_ref, d_ref):
    core = lax.rem(lax.axis_index("gx"), 2)
    for i in range(2):
        b_ref[i, pl.ds(pl.multiple_of(core * HALF, HALF), HALF)] = keep_ref[i]
        b_ref[i, pl.ds(pl.multiple_of((1 - core) * HALF, HALF), HALF)] = got_ref[i]
    first, last = b_ref[0], b_ref[1]
    s_ref[0:NY, :] = base_ref[0] + first
    for j in range(1, NX - 1):
        s_ref[j * NY : (j + 1) * NY, :] = base_ref[j] + gx_ref[j - 1] * first + hx_ref[j - 1] * last
    s_ref[(NX - 1) * NY : NX * NY, :] = base_ref[NX - 1] + last
    at = lambda y: s_ref[pl.ds(y, NX, stride=NY), :]
    mid = HALF
    low, high = at(0), at(NY - 1)
    for n in range(mid):
        y = n
        v_ref[y] = low * iy_ref[y]
        low = (at(y + 1) if y + 1 < mid else 0.0) + my_ref[y] * low
        y = NY - 1 - n
        if y > mid:
            v_ref[y] = high * iy_ref[y]
            high = (at(y - 1) if y - 1 > mid else 0.0) + my_ref[y] * high
    v = (at(mid) + low + high) * iy_ref[mid]
    low = high = v

    def emit(y, v):
        v_ref[y] = v
        d_ref[0, y * NX : (y + 1) * NX, :] = g_ref[y] * v
        d_ref[1, y * NX : (y + 1) * NX, :] = h_ref[y] * v

    emit(mid, v)
    for n in range(1, mid + 1):
        y = mid - n
        low = v_ref[y] + my_ref[y] * low
        emit(y, low)
        y = mid + n
        if y < NY:
            high = v_ref[y] + my_ref[y] * high
            emit(y, high)
    out_ref[...] = (
        port_ref[...]
        + lanes_to_rows(selector([(3, None)]), d_ref[0])
        + lanes_to_rows(selector([(4, None)]), d_ref[1])
    )


def z_local_kernel(k_ref, v_ref, y_ref):
    k2 = k_ref.reshape(ROWS, NZ)
    v2, y2 = v_ref.reshape(ROWS, NZ), y_ref.reshape(ROWS, NZ)

    def body(i, carry):
        y = i * STEP
        k = jnp.concatenate([k2[pl.ds(y + n, NX, stride=NY), :] for n in range(STEP)], axis=0)
        at = pl.ds(pl.multiple_of(y * NX, NX * STEP), NX * STEP)
        y2[at, :] = z_levels(k, v2[at, :])
        return carry

    lax.fori_loop(0, NY // STEP, body, 0)


def final_kernel(own_ref, one_ref, two_ref, three_ref, y_ref, g_ref, h_ref, u_ref, out_ref, held, nodes, b_ref):
    me = lax.axis_index("gz")
    ordered(me, (own_ref, one_ref, two_ref, three_ref), held)
    blocks = [[held[b, i : i + 1, :] for i in range(7)] for b in range(4)]
    e, c, r = chain_of(blocks, CZ)
    e[0] = e[0] + CZ * blocks[0][5]
    e[-1] = e[-1] + CZ * blocks[3][6]
    values = solve_chain(e, c, r)
    first, last = values[0], values[1]
    for b in range(1, 4):
        first = jnp.where(me == b, values[2 * b], first)
        last = jnp.where(me == b, values[2 * b + 1], last)
    row = lax.broadcasted_iota(jnp.int32, (8, ROWS), 0)
    both = jnp.where(row == 0, first, jnp.where(row == 1, last, 0.0))
    b_ref[0] = rows_to_lanes(both, selector([(0, None)]))
    b_ref[1] = rows_to_lanes(both, selector([(1, None)]))
    u2, out2 = u_ref.reshape(ROWS, NZ), out_ref.reshape(ROWS, NZ)
    for y in range(NY):
        at = pl.ds(y, NX, stride=NY)
        ys = slice(y * NX, (y + 1) * NX)
        out2[at, :] = u2[at, :] + 2.0 * (
            y_ref[y] + g_ref[y] * b_ref[0, ys, :] + h_ref[y] * b_ref[1, ys, :]
        )


def swap(block, axis, mask):
    n = lax.axis_size(axis)
    return lax.ppermute(block, axis, [(i, i ^ mask) for i in range(n)])


def per_device(u, k, f):
    edges, = call(edges_kernel, [(8, ROWS)], u, k, name="edges")
    one, two = swap(edges, "gz", 1), swap(edges, "gz", 3)
    rp, a, m, inv, ew = call(
        local_kernel,
        [(NX, NY, NZ), (NX - 2, NY, NZ), (NX - 2, NY, NZ), (NX - 2, NY, NZ), (3, NY, NZ)],
        u, k, f, name="local",
    )
    keep, send, rr = call(
        halo_kernel,
        [(7, HALF, NZ), (7, HALF, NZ), (NX - 2, NY, NZ)],
        edges, one, two, rp, a, m, ew, k, scratch=[(NX, NY, NZ)], name="halo",
    )
    got = swap(send, "gx", 1)
    chip, core_parts = call(core_kernel, [(7, HALF, NZ), (6, HALF, NZ)], keep, got, name="core")
    x_got = [swap(chip, "gx", 2 * i) for i in (1, 2, 3)]
    base, gx, hx, my, iy = call(
        prepare_kernel,
        [(NX, NY, NZ), (NX - 2, NY, NZ), (NX - 2, NY, NZ), (NY, NX, NZ), (NY, NX, NZ)],
        u, k, a, m, inv, rr, name="prepare",
    )
    group, chip_parts = call(
        chips_kernel, [(7, HALF, NZ), (18, HALF, NZ)], chip, *x_got, scratch=[(4, 7, HALF, NZ)], name="chips"
    )
    z_got = [swap(group, "gx", 8 * i) for i in (1, 2, 3)]
    gz, hz, port = call(
        z_ports_kernel,
        [(NY, NX, NZ), (NY, NX, NZ), (8, ROWS)],
        k, group, scratch=[(2, ROWS, NZ)], name="z_ports",
    )
    keep, send = call(
        back_kernel,
        [(2, HALF, NZ), (2, HALF, NZ)],
        group, *z_got, chip_parts, core_parts,
        scratch=[(4, 7, HALF, NZ), (8, HALF, NZ)], name="back",
    )
    got = swap(send, "gx", 1)
    v, message = call(
        y_kernel,
        [(NY, NX, NZ), (8, ROWS)],
        keep, got, base, gx, hx, my, iy, gz, hz, port,
        scratch=[(2, NY, NZ), (ROWS, NZ), (2, ROWS, NZ)], name="y_solve",
    )
    l_got = [swap(message, "gz", i) for i in (1, 2, 3)]
    yz, = call(z_local_kernel, [(NY, NX, NZ)], k, v, name="z_local")
    out, = call(
        final_kernel,
        [(NX, NY, NZ)],
        message, *l_got, yz, gz, hz, u,
        scratch=[(4, 8, ROWS), (8, ROWS), (2, ROWS, NZ)], name="final",
    )
    return out


def solution(mesh):
    spec = P("gx", None, "gz")
    return jax.shard_map(
        per_device, mesh=mesh, in_specs=(spec, spec, spec), out_specs=spec, check_vma=False
    )
```

```python
import functools

import jax
import jax.numpy as jnp
from jax import lax
from jax.experimental import pallas as pl
from jax.experimental.pallas import tpu as pltpu
from jax.sharding import PartitionSpec as P

NX, NY, NZ = 8, 64, 128
ROWS = NX * NY
HALF = NY // 2
CX = 0.25 * 16.0 * NX * NX
CY = 0.25 * 2.0
CZ = 0.25 * 0.5 * NZ * NZ
F32 = jnp.float32
VMEM_LIMIT = 24 * 1024 * 1024
HIGHEST = lax.Precision.HIGHEST


def call(kernel, outs, *args, scratch=(), sems=0, ins_in=pltpu.VMEM, outs_in=pltpu.VMEM, flops=0, name=None):
    shapes = [jax.ShapeDtypeStruct(s, F32) for s in outs]
    nbytes = sum(4 * a.size for a in args) + sum(4 * s.size for s in shapes)
    return pl.pallas_call(
        kernel,
        out_shape=shapes,
        in_specs=[pl.BlockSpec(memory_space=ins_in) for _ in args],
        out_specs=[pl.BlockSpec(memory_space=outs_in) for _ in outs],
        scratch_shapes=[pltpu.VMEM(s, F32) for s in scratch]
        + [pltpu.SemaphoreType.DMA] * sems,
        compiler_params=pltpu.CompilerParams(vmem_limit_bytes=VMEM_LIMIT),
        cost_estimate=pl.CostEstimate(flops=flops, bytes_accessed=nbytes, transcendentals=0),
        name=name,
    )(*args)


def lanes_to_rows(select, block):
    return lax.dot_general(
        select, block, (((1,), (1,)), ((), ())), precision=HIGHEST, preferred_element_type=F32
    )


def rows_to_lanes(rows, select):
    return lax.dot_general(
        rows, select, (((0,), (0,)), ((), ())), precision=HIGHEST, preferred_element_type=F32
    )


def selector(entries):
    row = lax.broadcasted_iota(jnp.int32, (8, NZ), 0)
    lane = lax.broadcasted_iota(jnp.int32, (8, NZ), 1)
    hit = None
    for r, l in entries:
        one = (row == r) if l is None else ((row == r) & (lane == l))
        hit = one if hit is None else (hit | one)
    return jnp.where(hit, 1.0, 0.0).astype(F32)


def reduce_chain(e, c, r):
    n = len(e)
    e_h, r_h = e[0], r[0]
    s, w, rr = e[1], c[0], r[1]
    parts = []
    for j in range(1, n - 1):
        inv = 1.0 / (s + w + c[j])
        a, m = w * inv, c[j] * inv
        parts.append((a, m, rr * inv))
        e_h = e_h + a * s
        r_h = r_h + a * rr
        s = e[j + 1] + m * s
        rr = r[j + 1] + m * rr
        w = m * w
    return (e_h, s, w, r_h, rr), parts


def expand_chain(first, last, parts):
    values = [last]
    for a, m, q in reversed(parts):
        values.append(q + a * first + m * values[-1])
    values.append(first)
    return values[::-1]


def solve_chain(e, c, r):
    n = len(e)
    s, rr = e[0], r[0]
    parts = []
    for j in range(n - 1):
        inv = 1.0 / (s + c[j])
        m = c[j] * inv
        parts.append((m, rr * inv))
        s = e[j + 1] + m * s
        rr = r[j + 1] + m * rr
    values = [rr / s]
    for m, q in reversed(parts):
        values.append(q + m * values[-1])
    return values[::-1]


def chain_of(blocks, scale):
    e, c, r = [], [], []
    for i, b in enumerate(blocks):
        e += [b[0], b[1]]
        r += [b[3], b[4]]
        c.append(b[2])
        if i + 1 < len(blocks):
            c.append(scale * (b[6] + blocks[i + 1][5]))
    return e, c, r


def edges_kernel(u_hbm, k_hbm, f_hbm, u_ref, k_ref, f_ref, out_ref, *sems):
    pairs = ((u_hbm, u_ref), (k_hbm, k_ref), (f_hbm, f_ref))
    copies = [pltpu.make_async_copy(a, b, sem) for (a, b), sem in zip(pairs, sems)]
    for copy in copies:
        copy.start()
    copies[0].wait()
    u = lanes_to_rows(selector([(0, 0), (1, NZ - 1)]), u_ref[...].reshape(ROWS, NZ))
    copies[1].wait()
    out_ref[...] = u + lanes_to_rows(
        selector([(2, 0), (3, NZ - 1)]), k_ref[...].reshape(ROWS, NZ)
    )
    copies[2].wait()


def local_kernel(u_ref, k_ref, f_ref, rp_ref, a_ref, m_ref, inv_ref, ew_ref):
    row = lax.broadcasted_iota(jnp.int32, (NY, NZ), 0)
    lane = lax.broadcasted_iota(jnp.int32, (NY, NZ), 1)
    for x in range(NX):
        u, k = u_ref[x], k_ref[x]
        flux_y = (CY * (k + pltpu.roll(k, NY - 1, 0))) * (pltpu.roll(u, NY - 1, 0) - u)
        flux_y = jnp.where(row == NY - 1, -(CY * k) * u, flux_y)
        low_y = jnp.where(row == 0, (CY * k) * u, pltpu.roll(flux_y, 1, 0))
        flux_z = (CZ * (k + pltpu.roll(k, NZ - 1, 1))) * (pltpu.roll(u, NZ - 1, 1) - u)
        flux_z = jnp.where(lane == NZ - 1, 0.0, flux_z)
        low_z = pltpu.roll(flux_z, 1, 1)
        rp_ref[x] = u + (flux_y - low_y) + (flux_z - low_z) + 0.5 * f_ref[x]
    s = jnp.ones((NY, NZ), F32)
    e_h = s
    w = CX * (k_ref[0] + k_ref[1])
    for j in range(1, NX - 1):
        c = CX * (k_ref[j] + k_ref[j + 1])
        inv = 1.0 / (s + w + c)
        a, m = w * inv, c * inv
        inv_ref[j - 1], a_ref[j - 1], m_ref[j - 1] = inv, a, m
        e_h = e_h + a * s
        s = 1.0 + m * s
        w = m * w
    ew_ref[0], ew_ref[1], ew_ref[2] = e_h, s, w


def halo_kernel(own_ref, one_ref, two_ref, rp_ref, a_ref, m_ref, ew_ref, k_ref, keep_ref, send_ref, rr_ref, fix_ref):
    g = lax.axis_index("gz")
    core = lax.rem(lax.axis_index("gx"), 2)
    odd = lax.rem(g, 2) == 1
    own, one, two = own_ref[...], one_ref[...], two_ref[...]
    low = jnp.where(odd, one, two) * jnp.where(g > 0, 1.0, 0.0)
    high = jnp.where(odd, two, one) * jnp.where(g < 3, 1.0, 0.0)
    at_low = CZ * (low[3:4] + own[2:3]) * (low[1:2] - own[0:1])
    at_high = CZ * (high[2:3] + own[3:4]) * (high[0:1] - own[1:2])
    row = lax.broadcasted_iota(jnp.int32, (8, ROWS), 0)
    both = jnp.where(row == 0, at_low, jnp.where(row == 1, at_high, 0.0))
    fix_ref[...] = rows_to_lanes(both, selector([(0, 0), (1, NZ - 1)])).reshape(NX, NY, NZ)
    for which, out in ((core, keep_ref), (1 - core, send_ref)):
        ys = pl.ds(pl.multiple_of(which * HALF, HALF), HALF)
        r_h = rp_ref[0, ys] + fix_ref[0, ys]
        rr = rp_ref[1, ys] + fix_ref[1, ys]
        for j in range(1, NX - 1):
            rr_ref[j - 1, ys] = rr
            r_h = r_h + a_ref[j - 1, ys] * rr
            rr = (rp_ref[j + 1, ys] + fix_ref[j + 1, ys]) + m_ref[j - 1, ys] * rr
        for i in range(3):
            out[i] = ew_ref[i, ys]
        out[3], out[4] = r_h, rr
        out[5], out[6] = k_ref[0, ys], k_ref[NX - 1, ys]


def core_kernel(own_ref, got_ref, out_ref, parts_ref):
    first = lax.rem(lax.axis_index("gx"), 2) == 0
    low = [jnp.where(first, own_ref[i], got_ref[i]) for i in range(7)]
    high = [jnp.where(first, got_ref[i], own_ref[i]) for i in range(7)]
    port, parts = reduce_chain(*chain_of([low, high], CX))
    for i, v in enumerate(port):
        out_ref[i] = v
    out_ref[5], out_ref[6] = low[5], high[6]
    for j, p in enumerate(parts):
        for i in range(3):
            parts_ref[3 * j + i] = p[i]


def ordered(me, refs, held):
    for i, ref in enumerate(refs):
        held[jnp.bitwise_xor(me, i)] = ref[...]
    return held


def chips_kernel(own_ref, one_ref, two_ref, three_ref, after_ref, also_ref, out_ref, parts_ref, held):
    me = lax.rem(lax.axis_index("gx") // 2, 4)
    ordered(me, (own_ref, one_ref, two_ref, three_ref), held)
    blocks = [[held[b, i] for i in range(7)] for b in range(4)]
    port, parts = reduce_chain(*chain_of(blocks, CX))
    for i, v in enumerate(port):
        out_ref[i] = v
    out_ref[5], out_ref[6] = blocks[0][5], blocks[3][6]
    for j, p in enumerate(parts):
        for i in range(3):
            parts_ref[3 * j + i] = p[i]


def back_kernel(own_ref, one_ref, two_ref, three_ref, chips_ref, cores_ref, after_ref, keep_ref, send_ref, held, nodes):
    index = lax.axis_index("gx")
    core, x, z = lax.rem(index, 2), lax.rem(index // 2, 4), index // 8
    ordered(z, (own_ref, one_ref, two_ref, three_ref), held)
    blocks = [[held[b, i] for i in range(7)] for b in range(4)]
    e, c, r = chain_of(blocks, CX)
    e[0] = e[0] + CX * blocks[0][5]
    e[-1] = e[-1] + CX * blocks[3][6]
    for i, v in enumerate(solve_chain(e, c, r)):
        nodes[i] = v
    first, last = nodes[2 * z], nodes[2 * z + 1]
    parts = [tuple(chips_ref[3 * j + i] for i in range(3)) for j in range(6)]
    for i, v in enumerate(expand_chain(first, last, parts)):
        nodes[i] = v
    first, last = nodes[2 * x], nodes[2 * x + 1]
    parts = [tuple(cores_ref[3 * j + i] for i in range(3)) for j in range(2)]
    v = expand_chain(first, last, parts)
    even = core == 0
    keep_ref[0], keep_ref[1] = jnp.where(even, v[0], v[2]), jnp.where(even, v[1], v[3])
    send_ref[0], send_ref[1] = jnp.where(even, v[2], v[0]), jnp.where(even, v[3], v[1])


def prepare_kernel(u_ref, k_ref, a_ref, m_ref, inv_ref, rr_ref, base_ref, g_ref, h_ref, my_ref, iy_ref):
    base_ref[0] = -u_ref[0]
    base_ref[NX - 1] = -u_ref[NX - 1]
    y = jnp.zeros((NY, NZ), F32)
    g = y
    h = jnp.ones((NY, NZ), F32)
    for j in range(NX - 2, 0, -1):
        m = m_ref[j - 1]
        y = rr_ref[j - 1] * inv_ref[j - 1] + m * y
        g = a_ref[j - 1] + m * g
        h = m * h
        base_ref[j], g_ref[j - 1], h_ref[j - 1] = y - u_ref[j], g, h
    k2 = k_ref.reshape(ROWS, NZ)
    at = lambda y: k2[pl.ds(y, NX, stride=NY), :]
    mid = HALF
    ends = []
    for start, step in ((0, 1), (NY - 1, -1)):
        k = at(start)
        ends.append([1.0 + CY * k, k, start, step])
    while any(e[2] != mid for e in ends):
        for e in ends:
            s, k, y, step = e
            if y == mid:
                continue
            k_next = at(y + step)
            c = CY * (k + k_next)
            inv = 1.0 / (s + c)
            m = c * inv
            my_ref[y], iy_ref[y] = m, inv
            e[0] = (0.0 if y + step == mid else 1.0) + m * s
            e[1], e[2] = k_next, y + step
    iy_ref[mid] = 1.0 / (1.0 + ends[0][0] + ends[1][0])
    my_ref[mid] = jnp.zeros((NX, NZ), F32)


LEVELS = 7
STEP = 16


def z_factors(k, keep):
    lane = lax.broadcasted_iota(jnp.int32, k.shape, 1)
    up = CZ * (k + pltpu.roll(k, NZ - 1, 1))
    low = pltpu.roll(up, 1, 1)
    top = up
    e = jnp.ones(k.shape, F32)
    for n in range(LEVELS):
        s = 1 << n
        inv = 1.0 / (e + low + up)
        has_low, has_up = lane >= s + 1, lane <= NZ - 2 - s
        low_in, up_in = jnp.where(has_low, low, 0.0), jnp.where(has_up, up, 0.0)
        keep(n, low_in, up_in, inv)
        share = e * inv
        e = e + low_in * pltpu.roll(share, s, 1) + up_in * pltpu.roll(share, NZ - s, 1)
        new_low = jnp.where(has_low, low * pltpu.roll(low * inv, s, 1), low)
        up = jnp.where(has_up, up * pltpu.roll(up * inv, NZ - s, 1), up)
        low = new_low
    inv = 1.0 / (e + low + up)
    first, last = lane == 0, lane == NZ - 1
    g = jnp.where(first, 1.0, jnp.where(last, 0.0, low * inv))
    h = jnp.where(first, 0.0, jnp.where(last, 1.0, up * inv))
    inv = jnp.where(first | last, 0.0, inv)
    return g, h, jnp.where(lane == NZ - 2, top * g, 0.0), inv


def z_ports_kernel(start, k_ref, after_ref, g_ref, h_ref, port_ref, f_ref, t_ref):
    del after_ref
    k2 = k_ref.reshape(ROWS, NZ)
    g2, h2 = g_ref.reshape(ROWS // 2, NZ), h_ref.reshape(ROWS // 2, NZ)

    def body(i, carry):
        y = start + i * STEP
        k = jnp.concatenate([k2[pl.ds(y + n, NX, stride=NY), :] for n in range(STEP)], axis=0)
        at = pl.ds(pl.multiple_of(i * (STEP * NX), NX * STEP), NX * STEP)

        def keep(n, *values):
            for j, v in enumerate(values):
                f_ref[3 * n + j, at, :] = v

        g, h, w, inv = z_factors(k, keep)
        f_ref[3 * LEVELS, at, :] = inv
        g2[at, :], h2[at, :] = g, h
        t_ref[0, at, :], t_ref[1, at, :] = k, w
        return carry

    lax.fori_loop(0, HALF // STEP, body, 0)
    port_ref[...] = (
        lanes_to_rows(selector([(0, None)]), g2[...])
        + lanes_to_rows(selector([(1, None)]), h2[...])
        + lanes_to_rows(selector([(2, None)]), t_ref[1])
        + lanes_to_rows(selector([(5, 0), (6, NZ - 1)]), t_ref[0])
    )


def y_kernel(keep_ref, got_ref, base_ref, gx_ref, hx_ref, my_ref, iy_ref, g0_ref, g1_ref, h0_ref, h1_ref, p0_ref, p1_ref, v_ref, out_ref, b_ref, s_ref, d_ref):
    core = lax.rem(lax.axis_index("gx"), 2)
    for i in range(2):
        b_ref[i, pl.ds(pl.multiple_of(core * HALF, HALF), HALF)] = keep_ref[i]
        b_ref[i, pl.ds(pl.multiple_of((1 - core) * HALF, HALF), HALF)] = got_ref[i]
    first, last = b_ref[0], b_ref[1]
    s_ref[0:NY, :] = base_ref[0] + first
    for j in range(1, NX - 1):
        s_ref[j * NY : (j + 1) * NY, :] = base_ref[j] + gx_ref[j - 1] * first + hx_ref[j - 1] * last
    s_ref[(NX - 1) * NY : NX * NY, :] = base_ref[NX - 1] + last
    at = lambda y: s_ref[pl.ds(y, NX, stride=NY), :]
    mid = HALF
    low, high = at(0), at(NY - 1)
    for n in range(mid):
        y = n
        v_ref[y] = low * iy_ref[y]
        low = (at(y + 1) if y + 1 < mid else 0.0) + my_ref[y] * low
        y = NY - 1 - n
        if y > mid:
            v_ref[y] = high * iy_ref[y]
            high = (at(y - 1) if y - 1 > mid else 0.0) + my_ref[y] * high
    v = (at(mid) + low + high) * iy_ref[mid]
    low = high = v

    def emit(y, v):
        v_ref[y] = v
        g, h = (g0_ref, h0_ref) if y < HALF else (g1_ref, h1_ref)
        d_ref[0, y * NX : (y + 1) * NX, :] = g[y % HALF] * v
        d_ref[1, y * NX : (y + 1) * NX, :] = h[y % HALF] * v

    emit(mid, v)
    for n in range(1, mid + 1):
        y = mid - n
        low = v_ref[y] + my_ref[y] * low
        emit(y, low)
        y = mid + n
        if y < NY:
            high = v_ref[y] + my_ref[y] * high
            emit(y, high)
    out_ref[...] = (
        jnp.concatenate([p0_ref[...], p1_ref[...]], axis=1)
        + lanes_to_rows(selector([(3, None)]), d_ref[0])
        + lanes_to_rows(selector([(4, None)]), d_ref[1])
    )


def z_local_kernel(f0_ref, f1_ref, v_ref, y_ref):
    v2, y2 = v_ref.reshape(ROWS, NZ), y_ref.reshape(ROWS, NZ)
    rows = STEP * NX

    for half, f_ref in enumerate((f0_ref, f1_ref)):

        def body(i, carry):
            at = pl.ds(pl.multiple_of(i * rows, rows), rows)
            full = pl.ds(pl.multiple_of(half * (ROWS // 2) + i * rows, rows), rows)
            r = v2[full, :]
            for n in range(LEVELS):
                s = 1 << n
                q = r * f_ref[3 * n + 2, at, :]
                r = (
                    r
                    + f_ref[3 * n, at, :] * pltpu.roll(q, s, 1)
                    + f_ref[3 * n + 1, at, :] * pltpu.roll(q, NZ - s, 1)
                )
            y2[full, :] = r * f_ref[3 * LEVELS, at, :]
            return carry

        lax.fori_loop(0, HALF // STEP, body, 0)


CHUNK = 16


def final_kernel(own_ref, one_ref, two_ref, three_ref, y_ref, g0_ref, g1_ref, h0_ref, h1_ref, u_ref, out_ref, held, b_ref, o_ref, *sems):
    me = lax.axis_index("gz")
    ordered(me, (own_ref, one_ref, two_ref, three_ref), held)
    blocks = [[held[b, i : i + 1, :] for i in range(7)] for b in range(4)]
    e, c, r = chain_of(blocks, CZ)
    e[0] = e[0] + CZ * blocks[0][5]
    e[-1] = e[-1] + CZ * blocks[3][6]
    values = solve_chain(e, c, r)
    first, last = values[0], values[1]
    for b in range(1, 4):
        first = jnp.where(me == b, values[2 * b], first)
        last = jnp.where(me == b, values[2 * b + 1], last)
    row = lax.broadcasted_iota(jnp.int32, (8, ROWS), 0)
    both = jnp.where(row == 0, first, jnp.where(row == 1, last, 0.0))
    b_ref[0] = rows_to_lanes(both, selector([(0, None)]))
    b_ref[1] = rows_to_lanes(both, selector([(1, None)]))
    u2, o2 = u_ref.reshape(ROWS, NZ), o_ref.reshape(ROWS, NZ)
    copies = []
    for y in range(NY):
        at = pl.ds(y, NX, stride=NY)
        ys = slice(y * NX, (y + 1) * NX)
        g, h = (g0_ref, h0_ref) if y < HALF else (g1_ref, h1_ref)
        o2[at, :] = u2[at, :] + 2.0 * (
            y_ref[y] + g[y % HALF] * b_ref[0, ys, :] + h[y % HALF] * b_ref[1, ys, :]
        )
        if y % CHUNK == CHUNK - 1:
            part = pl.ds(y + 1 - CHUNK, CHUNK)
            copies.append(pltpu.make_async_copy(o_ref.at[:, part], out_ref.at[:, part], sems[y // CHUNK]))
            copies[-1].start()
    for copy in copies:
        copy.wait()


def swap(block, axis, mask):
    n = lax.axis_size(axis)
    return lax.ppermute(block, axis, [(i, i ^ mask) for i in range(n)])


def per_device(u, k, f):
    u, k, f = (pltpu.with_memory_space_constraint(t, pltpu.HBM) for t in (u, k, f))
    u, k, f, edges = call(
        edges_kernel, [(NX, NY, NZ)] * 3 + [(8, ROWS)], u, k, f, sems=3, ins_in=pltpu.HBM, name="edges"
    )
    one, two = swap(edges, "gz", 1), swap(edges, "gz", 3)
    rp, a, m, inv, ew = call(
        local_kernel,
        [(NX, NY, NZ), (NX - 2, NY, NZ), (NX - 2, NY, NZ), (NX - 2, NY, NZ), (3, NY, NZ)],
        u, k, f, name="local",
    )
    keep, send, rr = call(
        halo_kernel,
        [(7, HALF, NZ), (7, HALF, NZ), (NX - 2, NY, NZ)],
        edges, one, two, rp, a, m, ew, k, scratch=[(NX, NY, NZ)], name="halo",
    )
    got = swap(send, "gx", 1)
    chip, core_parts = call(core_kernel, [(7, HALF, NZ), (6, HALF, NZ)], keep, got, name="core")
    x_got = [swap(chip, "gx", 2 * i) for i in (1, 2, 3)]
    base, gx, hx, my, iy = call(
        prepare_kernel,
        [(NX, NY, NZ), (NX - 2, NY, NZ), (NX - 2, NY, NZ), (NY, NX, NZ), (NY, NX, NZ)],
        u, k, a, m, inv, rr, name="prepare",
    )
    z_shapes = [(HALF, NX, NZ), (HALF, NX, NZ), (8, ROWS // 2), (3 * LEVELS + 1, ROWS // 2, NZ)]
    g0, h0, p0, f0 = call(
        functools.partial(z_ports_kernel, 0), z_shapes, k, chip, scratch=[(2, ROWS // 2, NZ)], name="z_ports"
    )
    group, chip_parts = call(
        chips_kernel,
        [(7, HALF, NZ), (18, HALF, NZ)],
        chip, *x_got, my, p0, scratch=[(4, 7, HALF, NZ)], name="chips",
    )
    z_got = [swap(group, "gx", 8 * i) for i in (1, 2, 3)]
    g1, h1, p1, f1 = call(
        functools.partial(z_ports_kernel, HALF), z_shapes, k, group, scratch=[(2, ROWS // 2, NZ)], name="z_ports"
    )
    keep, send = call(
        back_kernel,
        [(2, HALF, NZ), (2, HALF, NZ)],
        group, *z_got, chip_parts, core_parts, p1,
        scratch=[(4, 7, HALF, NZ), (8, HALF, NZ)], name="back",
    )
    got = swap(send, "gx", 1)
    v, message = call(
        y_kernel,
        [(NY, NX, NZ), (8, ROWS)],
        keep, got, base, gx, hx, my, iy, g0, g1, h0, h1, p0, p1,
        scratch=[(2, NY, NZ), (ROWS, NZ), (2, ROWS, NZ)], name="y_solve",
    )
    l_got = [swap(message, "gz", i) for i in (1, 2, 3)]
    yz, = call(z_local_kernel, [(NY, NX, NZ)], f0, f1, v, name="z_local")
    out, = call(
        final_kernel,
        [(NX, NY, NZ)],
        message, *l_got, yz, g0, g1, h0, h1, u,
        scratch=[(4, 8, ROWS), (2, ROWS, NZ), (NX, NY, NZ)], sems=NY // CHUNK,
        outs_in=pltpu.HBM, name="final",
    )
    return out


def solution(mesh):
    spec = P("gx", None, "gz")
    return jax.shard_map(
        per_device, mesh=mesh, in_specs=(spec, spec, spec), out_specs=spec, check_vma=False
    )
```

```python
import functools

import jax
import jax.numpy as jnp
from jax import lax
from jax.experimental import pallas as pl
from jax.experimental.pallas import tpu as pltpu
from jax.sharding import PartitionSpec as P

NX, NY, NZ = 8, 64, 128
ROWS = NX * NY
HALF = NY // 2
CX = 0.25 * 16.0 * NX * NX
CY = 0.25 * 2.0
CZ = 0.25 * 0.5 * NZ * NZ
F32 = jnp.float32
VMEM_LIMIT = 24 * 1024 * 1024
BF16 = jnp.bfloat16


def call(kernel, outs, *args, scratch=(), sems=0, ins_in=pltpu.VMEM, outs_in=pltpu.VMEM, flops=0, name=None):
    shapes = [jax.ShapeDtypeStruct(s, F32) for s in outs]
    nbytes = sum(4 * a.size for a in args) + sum(4 * s.size for s in shapes)
    return pl.pallas_call(
        kernel,
        out_shape=shapes,
        in_specs=[pl.BlockSpec(memory_space=ins_in) for _ in args],
        out_specs=[pl.BlockSpec(memory_space=outs_in) for _ in outs],
        scratch_shapes=[pltpu.VMEM(s, F32) for s in scratch]
        + [pltpu.SemaphoreType.DMA] * sems,
        compiler_params=pltpu.CompilerParams(vmem_limit_bytes=VMEM_LIMIT),
        cost_estimate=pl.CostEstimate(flops=flops, bytes_accessed=nbytes, transcendentals=0),
        name=name,
    )(*args)


def pieces(x):
    high = x.astype(BF16).astype(F32)
    rest = x - high
    middle = rest.astype(BF16).astype(F32)
    return high, middle, rest - middle


def lanes_to_rows(entries, block):
    high, middle, low = (p.astype(BF16) for p in pieces(block))
    select = selector(entries, 16, NZ).astype(BF16)
    dims = (((1,), (1,)), ((), ()))
    return lax.dot_general(
        jnp.concatenate([select, select], axis=1),
        jnp.concatenate([high, middle], axis=1),
        dims,
        preferred_element_type=F32,
    ) + lax.dot_general(select, low, dims, preferred_element_type=F32)


def rows_to_lanes(entries, rows, lanes):
    both = jnp.concatenate(pieces(rows) + (jnp.zeros_like(rows),), axis=0).astype(BF16)
    select = selector([(r + 8 * i, l) for i in range(3) for r, l in entries], 32, lanes)
    return lax.dot_general(
        both, select.astype(BF16), (((0,), (0,)), ((), ())), preferred_element_type=F32
    )


def selector(entries, rows, lanes):
    row = lax.broadcasted_iota(jnp.int32, (rows, lanes), 0)
    lane = lax.broadcasted_iota(jnp.int32, (rows, lanes), 1)
    hit = None
    for r, l in entries:
        one = row == r
        if isinstance(l, range):
            one = one & (lane >= l.start) & (lane < l.stop)
        elif l is not None:
            one = one & (lane == l)
        hit = one if hit is None else (hit | one)
    return jnp.where(hit, 1.0, 0.0).astype(F32)


def reduce_chain(e, c, r):
    n = len(e)
    e_h, r_h = e[0], r[0]
    s, w, rr = e[1], c[0], r[1]
    parts = []
    for j in range(1, n - 1):
        inv = 1.0 / (s + w + c[j])
        a, m = w * inv, c[j] * inv
        parts.append((a, m, rr * inv))
        e_h = e_h + a * s
        r_h = r_h + a * rr
        s = e[j + 1] + m * s
        rr = r[j + 1] + m * rr
        w = m * w
    return (e_h, s, w, r_h, rr), parts


def expand_chain(first, last, parts):
    values = [last]
    for a, m, q in reversed(parts):
        values.append(q + a * first + m * values[-1])
    values.append(first)
    return values[::-1]


def solve_chain(e, c, r):
    n = len(e)
    mid = n // 2
    low, high = [], []
    s, rr = e[0], r[0]
    t, tt = e[n - 1], r[n - 1]
    for j in range(mid):
        inv = 1.0 / (s + c[j])
        m = c[j] * inv
        low.append((m, rr * inv))
        s, rr = e[j + 1] + m * s, r[j + 1] + m * rr
        i = n - 1 - j
        if i > mid:
            inv = 1.0 / (t + c[i - 1])
            m = c[i - 1] * inv
            high.append((m, tt * inv))
            t, tt = m * t, m * tt
            if i - 1 > mid:
                t, tt = e[i - 1] + t, r[i - 1] + tt
    values = [None] * n
    values[mid] = (rr + tt) / (s + t)
    for j in range(mid - 1, -1, -1):
        m, q = low[j]
        values[j] = q + m * values[j + 1]
    for i in range(mid + 1, n):
        m, q = high[n - 1 - i]
        values[i] = q + m * values[i - 1]
    return values


def join(blocks):
    e = [blocks[0][0]]
    r = [blocks[0][3]]
    for i, b in enumerate(blocks):
        e.append(b[1] + blocks[i + 1][0] if i + 1 < len(blocks) else b[1])
        r.append(b[4] + blocks[i + 1][3] if i + 1 < len(blocks) else b[4])
    return e, [b[2] for b in blocks], r


def edges_kernel(u_hbm, k_hbm, f_hbm, u_ref, k_ref, f_ref, out_ref, end_ref, *sems):
    pairs = ((k_hbm, k_ref), (u_hbm, u_ref), (f_hbm, f_ref))
    copies = [pltpu.make_async_copy(a, b, sem) for (a, b), sem in zip(pairs, sems)]
    for copy in copies:
        copy.start()
    lane = lax.broadcasted_iota(jnp.int32, (ROWS, NZ), 1)
    copies[0].wait()
    k = pltpu.roll(k_ref[...].reshape(ROWS, NZ), 2, 1)
    copies[1].wait()
    both = jnp.where((lane == 1) | (lane == 2), k, u_ref[...].reshape(ROWS, NZ))
    out_ref[...] = lanes_to_rows([(0, 0), (1, NZ - 1), (2, 2), (3, 1)], both)[:8]
    end_ref[...] = k_ref[NX - 1]
    copies[2].wait()


def local_kernel(u_ref, k_ref, f_ref, rp_ref, a_ref, m_ref, inv_ref, ew_ref):
    row = lax.broadcasted_iota(jnp.int32, (NY, NZ), 0)
    lane = lax.broadcasted_iota(jnp.int32, (NY, NZ), 1)
    for x in range(NX):
        u, k = u_ref[x], k_ref[x]
        flux_y = (CY * (k + pltpu.roll(k, NY - 1, 0))) * (pltpu.roll(u, NY - 1, 0) - u)
        flux_y = jnp.where(row == NY - 1, -(CY * k) * u, flux_y)
        low_y = jnp.where(row == 0, (CY * k) * u, pltpu.roll(flux_y, 1, 0))
        flux_z = (CZ * (k + pltpu.roll(k, NZ - 1, 1))) * (pltpu.roll(u, NZ - 1, 1) - u)
        flux_z = jnp.where(lane == NZ - 1, 0.0, flux_z)
        low_z = pltpu.roll(flux_z, 1, 1)
        rp_ref[x] = u + (flux_y - low_y) + (flux_z - low_z) + 0.5 * f_ref[x]
    s = jnp.ones((NY, NZ), F32)
    e_h = s
    w = CX * (k_ref[0] + k_ref[1])
    for j in range(1, NX - 1):
        c = CX * (k_ref[j] + k_ref[j + 1])
        inv = 1.0 / (s + w + c)
        a, m = w * inv, c * inv
        inv_ref[j - 1], a_ref[j - 1], m_ref[j - 1] = inv, a, m
        e_h = e_h + a * s
        s = 1.0 + m * s
        w = m * w
    ew_ref[0], ew_ref[1], ew_ref[2] = e_h, s, w


def halo_kernel(own_ref, one_ref, two_ref, below_ref, rp_ref, a_ref, m_ref, ew_ref, k_ref, keep_ref, send_ref, rr_ref, fix_ref):
    g = lax.axis_index("gz")
    index = lax.axis_index("gx")
    core = lax.rem(index, 2)
    odd = lax.rem(g, 2) == 1
    own, one, two = own_ref[...], one_ref[...], two_ref[...]
    low = jnp.where(odd, one, two) * jnp.where(g > 0, 1.0, 0.0)
    high = jnp.where(odd, two, one) * jnp.where(g < 3, 1.0, 0.0)
    at_low = CZ * (low[3:4] + own[2:3]) * (low[1:2] - own[0:1])
    at_high = CZ * (high[2:3] + own[3:4]) * (high[0:1] - own[1:2])
    row = lax.broadcasted_iota(jnp.int32, (8, ROWS), 0)
    both = jnp.where(row == 0, at_low, jnp.where(row == 1, at_high, 0.0))
    fix_ref[...] = rows_to_lanes([(0, 0), (1, NZ - 1)], both, NZ).reshape(NX, NY, NZ)
    top = jnp.where(index == lax.axis_size("gx") - 1, CX, 0.0)
    inner = jnp.where(core == 0, NX - 1, 0)
    for which, out in ((core, keep_ref), (1 - core, send_ref)):
        ys = pl.ds(pl.multiple_of(which * HALF, HALF), HALF)
        r_h = rp_ref[0, ys] + fix_ref[0, ys]
        rr = rp_ref[1, ys] + fix_ref[1, ys]
        for j in range(1, NX - 1):
            rr_ref[j - 1, ys] = rr
            r_h = r_h + a_ref[j - 1, ys] * rr
            rr = (rp_ref[j + 1, ys] + fix_ref[j + 1, ys]) + m_ref[j - 1, ys] * rr
        out[0], out[2] = ew_ref[0, ys], ew_ref[2, ys]
        out[1] = ew_ref[1, ys] + top * k_ref[NX - 1, ys]
        out[3], out[4] = r_h, rr
        out[5] = k_ref[inner, ys]
        out[6] = CX * (below_ref[ys] + k_ref[0, ys])


def core_kernel(own_ref, got_ref, out_ref, parts_ref):
    first = lax.rem(lax.axis_index("gx"), 2) == 0
    low = [jnp.where(first, own_ref[i], got_ref[i]) for i in range(7)]
    high = [jnp.where(first, got_ref[i], own_ref[i]) for i in range(6)]
    e = [0.0, low[0], low[1], high[0], high[1]]
    c = [low[6], low[2], CX * (low[5] + high[5]), high[2]]
    r = [0.0, low[3], low[4], high[3], high[4]]
    port, parts = reduce_chain(e, c, r)
    for i, v in enumerate(port):
        out_ref[i] = v
    for j, p in enumerate(parts):
        for i in range(3):
            parts_ref[3 * j + i] = p[i]


def ordered(me, refs, held):
    for i, ref in enumerate(refs):
        held[jnp.bitwise_xor(me, i)] = ref[...]
    return held


def chips_kernel(own_ref, one_ref, two_ref, three_ref, after_ref, also_ref, out_ref, parts_ref, held):
    del after_ref, also_ref
    me = lax.rem(lax.axis_index("gx") // 2, 4)
    ordered(me, (own_ref, one_ref, two_ref, three_ref), held)
    blocks = [[held[b, i] for i in range(5)] for b in range(4)]
    port, parts = reduce_chain(*join(blocks))
    for i, v in enumerate(port):
        out_ref[i] = v
    for j, p in enumerate(parts):
        for i in range(3):
            parts_ref[3 * j + i] = p[i]


def back_kernel(own_ref, one_ref, two_ref, three_ref, chips_ref, cores_ref, after_ref, keep_ref, send_ref, held, nodes):
    del after_ref
    index = lax.axis_index("gx")
    core, x, z = lax.rem(index, 2), lax.rem(index // 2, 4), index // 8
    ordered(z, (own_ref, one_ref, two_ref, three_ref), held)
    blocks = [[held[b, i] for i in range(5)] for b in range(4)]
    e, c, r = join(blocks)
    e[1] = e[1] + c[0]
    nodes[0] = jnp.zeros((HALF, NZ), F32)
    for i, v in enumerate(solve_chain(e[1:], c[1:], r[1:])):
        nodes[i + 1] = v
    first, last = nodes[z], nodes[z + 1]
    parts = [tuple(chips_ref[3 * j + i] for i in range(3)) for j in range(3)]
    for i, v in enumerate(expand_chain(first, last, parts)):
        nodes[i] = v
    first, last = nodes[x], nodes[x + 1]
    parts = [tuple(cores_ref[3 * j + i] for i in range(3)) for j in range(3)]
    v = expand_chain(first, last, parts)
    even = core == 0
    keep_ref[0], keep_ref[1] = jnp.where(even, v[1], v[3]), jnp.where(even, v[2], v[4])
    send_ref[0], send_ref[1] = jnp.where(even, v[3], v[1]), jnp.where(even, v[4], v[2])


def y_major(ref, x, block):
    rows = ref.reshape(ROWS, NZ)
    for t in range(NY // 8):
        rows[pl.ds(t * 8 * NX + x, 8, stride=NX), :] = block[8 * t : 8 * t + 8]


def prepare_kernel(u_ref, k_ref, a_ref, m_ref, inv_ref, rr_ref, base_ref, g_ref, h_ref, my_ref, iy_ref):
    zero = jnp.zeros((NY, NZ), F32)
    y, g, h = zero, zero, zero + 1.0
    y_major(base_ref, NX - 1, -u_ref[NX - 1])
    y_major(g_ref, NX - 1, g)
    y_major(h_ref, NX - 1, h)
    for j in range(NX - 2, 0, -1):
        m = m_ref[j - 1]
        y = rr_ref[j - 1] * inv_ref[j - 1] + m * y
        g = a_ref[j - 1] + m * g
        h = m * h
        y_major(base_ref, j, y - u_ref[j])
        y_major(g_ref, j, g)
        y_major(h_ref, j, h)
    y_major(base_ref, 0, -u_ref[0])
    y_major(g_ref, 0, zero + 1.0)
    y_major(h_ref, 0, zero)
    k2 = k_ref.reshape(ROWS, NZ)
    at = lambda y: k2[pl.ds(y, NX, stride=NY), :]
    mid = HALF
    ends = []
    for start, step in ((0, 1), (NY - 1, -1)):
        k = at(start)
        ends.append([1.0 + CY * k, k, start, step])
    while any(e[2] != mid for e in ends):
        for e in ends:
            s, k, y, step = e
            if y == mid:
                continue
            k_next = at(y + step)
            c = CY * (k + k_next)
            inv = 1.0 / (s + c)
            m = c * inv
            my_ref[y], iy_ref[y] = m, inv
            e[0] = (0.0 if y + step == mid else 1.0) + m * s
            e[1], e[2] = k_next, y + step
    iy_ref[mid] = 1.0 / (1.0 + ends[0][0] + ends[1][0])
    my_ref[mid] = jnp.zeros((NX, NZ), F32)


LEVELS = 7
STEP = 32


def z_factors(k, keep):
    lane = lax.broadcasted_iota(jnp.int32, k.shape, 1)
    up = CZ * (k + pltpu.roll(k, NZ - 1, 1))
    low = pltpu.roll(up, 1, 1)
    top = up
    e = jnp.ones(k.shape, F32)
    for n in range(LEVELS):
        s = 1 << n
        inv = 1.0 / (e + low + up)
        has_low, has_up = lane >= s + 1, lane <= NZ - 2 - s
        low_in, up_in = jnp.where(has_low, low, 0.0), jnp.where(has_up, up, 0.0)
        keep(n, low_in, up_in, inv)
        share = e * inv
        e = e + low_in * pltpu.roll(share, s, 1) + up_in * pltpu.roll(share, NZ - s, 1)
        new_low = jnp.where(has_low, low * pltpu.roll(low * inv, s, 1), low)
        up = jnp.where(has_up, up * pltpu.roll(up * inv, NZ - s, 1), up)
        low = new_low
    inv = 1.0 / (e + low + up)
    first, last = lane == 0, lane == NZ - 1
    g = jnp.where(first, 1.0, jnp.where(last, 0.0, low * inv))
    h = jnp.where(first, 0.0, jnp.where(last, 1.0, up * inv))
    inv = jnp.where(first | last, 0.0, inv)
    return g, h, jnp.where(lane == NZ - 2, top * g, 0.0), inv


def z_ports_kernel(start, k_ref, u_ref, after_ref, uy_ref, g_ref, h_ref, port_ref, f_ref, t_ref):
    del after_ref
    k2, u2 = k_ref.reshape(ROWS, NZ), u_ref.reshape(ROWS, NZ)
    for y in range(HALF):
        uy_ref[y] = u2[pl.ds(start + y, NX, stride=NY), :]
    g2, h2 = g_ref.reshape(ROWS // 2, NZ), h_ref.reshape(ROWS // 2, NZ)

    def body(i, carry):
        y = start + i * STEP
        k = jnp.concatenate([k2[pl.ds(y + n, NX, stride=NY), :] for n in range(STEP)], axis=0)
        at = pl.ds(pl.multiple_of(i * (STEP * NX), NX * STEP), NX * STEP)

        def keep(n, *values):
            for j, v in enumerate(values):
                f_ref[3 * n + j, at, :] = v

        g, h, w, inv = z_factors(k, keep)
        f_ref[3 * LEVELS, at, :] = inv
        g2[at, :], h2[at, :] = g, h
        t_ref[0, at, :], t_ref[1, at, :] = k, w
        return carry

    lax.fori_loop(0, HALF // STEP, body, 0)
    port_ref[...] = (
        lanes_to_rows([(0, None)], g2[...])
        + lanes_to_rows([(1, None)], h2[...])
        + lanes_to_rows([(2, NZ - 2)], t_ref[1])
        + lanes_to_rows([(5, 0), (6, NZ - 1)], t_ref[0])
    )[:8]


def y_kernel(keep_ref, got_ref, base_ref, gx_ref, hx_ref, my_ref, iy_ref, g0_ref, g1_ref, h0_ref, h1_ref, p0_ref, p1_ref, v_ref, out_ref, b_ref, d_ref):
    core = lax.rem(lax.axis_index("gx"), 2)
    for i in range(2):
        b_ref[i, pl.ds(pl.multiple_of(core * HALF, HALF), HALF)] = keep_ref[i]
        b_ref[i, pl.ds(pl.multiple_of((1 - core) * HALF, HALF), HALF)] = got_ref[i]

    def at(y):
        first = jnp.broadcast_to(b_ref[0, y : y + 1, :], (NX, NZ))
        last = jnp.broadcast_to(b_ref[1, y : y + 1, :], (NX, NZ))
        return base_ref[y] + gx_ref[y] * first + hx_ref[y] * last

    mid = HALF
    low, high = at(0), at(NY - 1)
    for n in range(mid):
        y = n
        v_ref[y] = low * iy_ref[y]
        low = (at(y + 1) if y + 1 < mid else 0.0) + my_ref[y] * low
        y = NY - 1 - n
        if y > mid:
            v_ref[y] = high * iy_ref[y]
            high = (at(y - 1) if y - 1 > mid else 0.0) + my_ref[y] * high
    v = (at(mid) + low + high) * iy_ref[mid]
    low = high = v

    def emit(y, v):
        v_ref[y] = v
        g, h = (g0_ref, h0_ref) if y < HALF else (g1_ref, h1_ref)
        d_ref[0, y * NX : (y + 1) * NX, :] = g[y % HALF] * v
        d_ref[1, y * NX : (y + 1) * NX, :] = h[y % HALF] * v

    emit(mid, v)
    for n in range(1, mid + 1):
        y = mid - n
        low = v_ref[y] + my_ref[y] * low
        emit(y, low)
        y = mid + n
        if y < NY:
            high = v_ref[y] + my_ref[y] * high
            emit(y, high)
    out_ref[...] = (
        jnp.concatenate([p0_ref[...], p1_ref[...]], axis=1)
        + (lanes_to_rows([(3, None)], d_ref[0]) + lanes_to_rows([(4, None)], d_ref[1]))[:8]
    )


def z_local_kernel(f0_ref, f1_ref, u0_ref, u1_ref, v_ref, y_ref):
    v2, y2 = v_ref.reshape(ROWS, NZ), y_ref.reshape(ROWS, NZ)
    rows = STEP * NX

    for half, (f_ref, u_ref) in enumerate(((f0_ref, u0_ref), (f1_ref, u1_ref))):
        u2 = u_ref.reshape(ROWS // 2, NZ)

        def body(i, carry):
            at = pl.ds(pl.multiple_of(i * rows, rows), rows)
            full = pl.ds(pl.multiple_of(half * (ROWS // 2) + i * rows, rows), rows)
            r = v2[full, :]
            for n in range(LEVELS):
                s = 1 << n
                q = r * f_ref[3 * n + 2, at, :]
                r = (
                    r
                    + f_ref[3 * n, at, :] * pltpu.roll(q, s, 1)
                    + f_ref[3 * n + 1, at, :] * pltpu.roll(q, NZ - s, 1)
                )
            y2[full, :] = u2[at, :] + 2.0 * (r * f_ref[3 * LEVELS, at, :])
            return carry

        lax.fori_loop(0, HALF // STEP, body, 0)


CHUNK = 16


def final_kernel(own_ref, one_ref, two_ref, three_ref, y_ref, g0_ref, g1_ref, h0_ref, h1_ref, out_ref, held, b_ref, o_ref, *sems):
    me = lax.axis_index("gz")
    ordered(me, (own_ref, one_ref, two_ref, three_ref), held)
    blocks = [[held[b, i : i + 1, :] for i in range(7)] for b in range(4)]
    e, c, r = [], [], []
    for i, b in enumerate(blocks):
        e += [b[0], b[1]]
        r += [b[3], b[4]]
        c.append(b[2])
        if i < 3:
            c.append(CZ * (b[6] + blocks[i + 1][5]))
    e[0] = e[0] + CZ * blocks[0][5]
    e[-1] = e[-1] + CZ * blocks[3][6]
    values = solve_chain(e, c, r)
    first, last = values[0], values[1]
    for b in range(1, 4):
        first = jnp.where(me == b, values[2 * b], first)
        last = jnp.where(me == b, values[2 * b + 1], last)
    row = lax.broadcasted_iota(jnp.int32, (8, ROWS), 0)
    both = jnp.where(row == 0, 2.0 * first, jnp.where(row == 1, 2.0 * last, 0.0))
    b_ref[...] = rows_to_lanes([(0, range(0, NZ)), (1, range(NZ, 2 * NZ))], both, 2 * NZ)
    o2 = o_ref.reshape(ROWS, NZ)
    copies = []
    for y in range(NY):
        ys = slice(y * NX, (y + 1) * NX)
        g, h = (g0_ref, h0_ref) if y < HALF else (g1_ref, h1_ref)
        o2[pl.ds(y, NX, stride=NY), :] = (
            y_ref[y] + g[y % HALF] * b_ref[ys, :NZ] + h[y % HALF] * b_ref[ys, NZ:]
        )
        if y % CHUNK == CHUNK - 1:
            part = pl.ds(y + 1 - CHUNK, CHUNK)
            copies.append(pltpu.make_async_copy(o_ref.at[:, part], out_ref.at[:, part], sems[y // CHUNK]))
            copies[-1].start()
    for copy in copies:
        copy.wait()


def swap(block, axis, mask):
    n = lax.axis_size(axis)
    return lax.ppermute(block, axis, [(i, i ^ mask) for i in range(n)])


def per_device(u, k, f):
    n = lax.axis_size("gx")
    u, k, f = (pltpu.with_memory_space_constraint(t, pltpu.HBM) for t in (u, k, f))
    u, k, f, edges, end = call(
        edges_kernel,
        [(NX, NY, NZ)] * 3 + [(8, ROWS), (NY, NZ)],
        u, k, f, sems=3, ins_in=pltpu.HBM, name="edges",
    )
    one, two = swap(edges, "gz", 1), swap(edges, "gz", 3)
    below = lax.ppermute(end, "gx", [(i, i + 1) for i in range(1, n - 1, 2)])
    rp, a, m, inv, ew = call(
        local_kernel,
        [(NX, NY, NZ), (NX - 2, NY, NZ), (NX - 2, NY, NZ), (NX - 2, NY, NZ), (3, NY, NZ)],
        u, k, f, name="local",
    )
    keep, send, rr = call(
        halo_kernel,
        [(7, HALF, NZ), (7, HALF, NZ), (NX - 2, NY, NZ)],
        edges, one, two, below, rp, a, m, ew, k, scratch=[(NX, NY, NZ)], name="halo",
    )
    got = swap(send, "gx", 1)
    chip, core_parts = call(core_kernel, [(5, HALF, NZ), (9, HALF, NZ)], keep, got, name="core")
    x_got = [swap(chip, "gx", 2 * i) for i in (1, 2, 3)]
    base, gx, hx, my, iy = call(
        prepare_kernel, [(NY, NX, NZ)] * 5, u, k, a, m, inv, rr, name="prepare"
    )
    z_shapes = [(HALF, NX, NZ)] * 3 + [(8, ROWS // 2), (3 * LEVELS + 1, ROWS // 2, NZ)]
    u0, g0, h0, p0, f0 = call(
        functools.partial(z_ports_kernel, 0),
        z_shapes, k, u, chip, scratch=[(2, ROWS // 2, NZ)], name="z_ports",
    )
    group, chip_parts = call(
        chips_kernel,
        [(5, HALF, NZ), (9, HALF, NZ)],
        chip, *x_got, my, p0, scratch=[(4, 5, HALF, NZ)], name="chips",
    )
    z_got = [swap(group, "gx", 8 * i) for i in (1, 2, 3)]
    u1, g1, h1, p1, f1 = call(
        functools.partial(z_ports_kernel, HALF),
        z_shapes, k, u, group, scratch=[(2, ROWS // 2, NZ)], name="z_ports",
    )
    keep, send = call(
        back_kernel,
        [(2, HALF, NZ), (2, HALF, NZ)],
        group, *z_got, chip_parts, core_parts, p1,
        scratch=[(4, 5, HALF, NZ), (5, HALF, NZ)], name="back",
    )
    got = swap(send, "gx", 1)
    v, message = call(
        y_kernel,
        [(NY, NX, NZ), (8, ROWS)],
        keep, got, base, gx, hx, my, iy, g0, g1, h0, h1, p0, p1,
        scratch=[(2, NY, NZ), (2, ROWS, NZ)], name="y_solve",
    )
    l_got = [swap(message, "gz", i) for i in (1, 2, 3)]
    yz, = call(z_local_kernel, [(NY, NX, NZ)], f0, f1, u0, u1, v, name="z_local")
    out, = call(
        final_kernel,
        [(NX, NY, NZ)],
        message, *l_got, yz, g0, g1, h0, h1,
        scratch=[(4, 8, ROWS), (ROWS, 2 * NZ), (NX, NY, NZ)], sems=NY // CHUNK,
        outs_in=pltpu.HBM, name="final",
    )
    return out


def solution(mesh):
    spec = P("gx", None, "gz")
    return jax.shard_map(
        per_device, mesh=mesh, in_specs=(spec, spec, spec), out_specs=spec, check_vma=False
    )
```

```python
import functools

import jax
import jax.numpy as jnp
from jax import lax
from jax.experimental import pallas as pl
from jax.experimental.pallas import tpu as pltpu
from jax.sharding import PartitionSpec as P

NX, NY, NZ = 8, 64, 128
ROWS = NX * NY
HALF = NY // 2
X_ORDER, Z_ORDER, L_ORDER = (2, 3, 1), (2, 3, 1), (2, 3, 1)
RING = 8
CX = 0.25 * 16.0 * NX * NX
CY = 0.25 * 2.0
CZ = 0.25 * 0.5 * NZ * NZ
F32 = jnp.float32
VMEM_LIMIT = 24 * 1024 * 1024
BF16 = jnp.bfloat16


def call(kernel, outs, *args, scratch=(), sems=0, ins_in=pltpu.VMEM, outs_in=pltpu.VMEM, flops=0, name=None):
    shapes = [jax.ShapeDtypeStruct(s, F32) for s in outs]
    nbytes = sum(4 * a.size for a in args) + sum(4 * s.size for s in shapes)
    return pl.pallas_call(
        kernel,
        out_shape=shapes,
        in_specs=[pl.BlockSpec(memory_space=ins_in) for _ in args],
        out_specs=[pl.BlockSpec(memory_space=outs_in) for _ in outs],
        scratch_shapes=[pltpu.VMEM(s, F32) for s in scratch]
        + [pltpu.SemaphoreType.DMA] * sems,
        compiler_params=pltpu.CompilerParams(vmem_limit_bytes=VMEM_LIMIT),
        cost_estimate=pl.CostEstimate(flops=flops, bytes_accessed=nbytes, transcendentals=0),
        name=name,
    )(*args)


def pieces(x):
    high = x.astype(BF16).astype(F32)
    rest = x - high
    middle = rest.astype(BF16).astype(F32)
    return high, middle, rest - middle


def lanes_to_rows(entries, block):
    high, middle, low = (p.astype(BF16) for p in pieces(block))
    select = selector(entries, 16, NZ).astype(BF16)
    dims = (((1,), (1,)), ((), ()))
    return lax.dot_general(
        jnp.concatenate([select, select], axis=1),
        jnp.concatenate([high, middle], axis=1),
        dims,
        preferred_element_type=F32,
    ) + lax.dot_general(select, low, dims, preferred_element_type=F32)


def rows_to_lanes(entries, rows, lanes):
    both = jnp.concatenate(pieces(rows) + (jnp.zeros_like(rows),), axis=0).astype(BF16)
    select = selector([(r + 8 * i, l) for i in range(3) for r, l in entries], 32, lanes)
    return lax.dot_general(
        both, select.astype(BF16), (((0,), (0,)), ((), ())), preferred_element_type=F32
    )


def selector(entries, rows, lanes):
    row = lax.broadcasted_iota(jnp.int32, (rows, lanes), 0)
    lane = lax.broadcasted_iota(jnp.int32, (rows, lanes), 1)
    hit = None
    for r, l in entries:
        one = row == r
        if isinstance(l, range):
            one = one & (lane >= l.start) & (lane < l.stop)
        elif l is not None:
            one = one & (lane == l)
        hit = one if hit is None else (hit | one)
    return jnp.where(hit, 1.0, 0.0).astype(F32)


def reduce_chain(e, c, r):
    n = len(e)
    e_h, r_h = e[0], r[0]
    s, w, rr = e[1], c[0], r[1]
    parts = []
    for j in range(1, n - 1):
        inv = 1.0 / (s + w + c[j])
        a, m = w * inv, c[j] * inv
        parts.append((a, m, rr * inv))
        e_h = e_h + a * s
        r_h = r_h + a * rr
        s = e[j + 1] + m * s
        rr = r[j + 1] + m * rr
        w = m * w
    return (e_h, s, w, r_h, rr), parts


def expand_chain(first, last, parts):
    values = [last]
    for a, m, q in reversed(parts):
        values.append(q + a * first + m * values[-1])
    values.append(first)
    return values[::-1]


def solve_chain(e, c, r):
    n = len(e)
    mid = n // 2
    low, high = [], []
    s, rr = e[0], r[0]
    t, tt = e[n - 1], r[n - 1]
    for j in range(mid):
        inv = 1.0 / (s + c[j])
        m = c[j] * inv
        low.append((m, rr * inv))
        s, rr = e[j + 1] + m * s, r[j + 1] + m * rr
        i = n - 1 - j
        if i > mid:
            inv = 1.0 / (t + c[i - 1])
            m = c[i - 1] * inv
            high.append((m, tt * inv))
            t, tt = m * t, m * tt
            if i - 1 > mid:
                t, tt = e[i - 1] + t, r[i - 1] + tt
    values = [None] * n
    values[mid] = (rr + tt) / (s + t)
    for j in range(mid - 1, -1, -1):
        m, q = low[j]
        values[j] = q + m * values[j + 1]
    for i in range(mid + 1, n):
        m, q = high[n - 1 - i]
        values[i] = q + m * values[i - 1]
    return values


def join(blocks):
    e = [blocks[0][0]]
    r = [blocks[0][3]]
    for i, b in enumerate(blocks):
        e.append(b[1] + blocks[i + 1][0] if i + 1 < len(blocks) else b[1])
        r.append(b[4] + blocks[i + 1][3] if i + 1 < len(blocks) else b[4])
    return e, [b[2] for b in blocks], r


def edges_kernel(u_hbm, k_hbm, f_hbm, u_ref, k_ref, f_ref, out_ref, end_ref, *sems):
    pairs = ((k_hbm, k_ref), (u_hbm, u_ref), (f_hbm, f_ref))
    copies = [pltpu.make_async_copy(a, b, sem) for (a, b), sem in zip(pairs, sems)]
    for copy in copies:
        copy.start()
    lane = lax.broadcasted_iota(jnp.int32, (ROWS, NZ), 1)
    copies[0].wait()
    k = pltpu.roll(k_ref[...].reshape(ROWS, NZ), 2, 1)
    copies[1].wait()
    both = jnp.where((lane == 1) | (lane == 2), k, u_ref[...].reshape(ROWS, NZ))
    out_ref[...] = lanes_to_rows([(0, 0), (1, NZ - 1), (2, 2), (3, 1)], both)[:8]
    index = lax.axis_index("gx")
    end_ref[...] = k_ref[jnp.where(lax.rem(index, 2) == 1, NX - 1, 0)]
    copies[2].wait()


def local_kernel(u_ref, k_ref, f_ref, rp_ref, a_ref, m_ref, inv_ref, ew_ref):
    row = lax.broadcasted_iota(jnp.int32, (NY, NZ), 0)
    lane = lax.broadcasted_iota(jnp.int32, (NY, NZ), 1)
    for x in range(NX):
        u, k = u_ref[x], k_ref[x]
        flux_y = (CY * (k + pltpu.roll(k, NY - 1, 0))) * (pltpu.roll(u, NY - 1, 0) - u)
        flux_y = jnp.where(row == NY - 1, -(CY * k) * u, flux_y)
        low_y = jnp.where(row == 0, (CY * k) * u, pltpu.roll(flux_y, 1, 0))
        flux_z = (CZ * (k + pltpu.roll(k, NZ - 1, 1))) * (pltpu.roll(u, NZ - 1, 1) - u)
        flux_z = jnp.where(lane == NZ - 1, 0.0, flux_z)
        low_z = pltpu.roll(flux_z, 1, 1)
        rp_ref[x] = u + (flux_y - low_y) + (flux_z - low_z) + 0.5 * f_ref[x]
    s = jnp.ones((NY, NZ), F32)
    e_h = s
    w = CX * (k_ref[0] + k_ref[1])
    for j in range(1, NX - 1):
        c = CX * (k_ref[j] + k_ref[j + 1])
        inv = 1.0 / (s + w + c)
        a, m = w * inv, c * inv
        inv_ref[j - 1], a_ref[j - 1], m_ref[j - 1] = inv, a, m
        e_h = e_h + a * s
        s = 1.0 + m * s
        w = m * w
    ew_ref[0], ew_ref[1], ew_ref[2] = e_h, s, w


def halo_kernel(own_ref, one_ref, two_ref, below_ref, rp_ref, a_ref, m_ref, ew_ref, k_ref, keep_ref, send_ref, rr_ref, fix_ref):
    g = lax.axis_index("gz")
    index = lax.axis_index("gx")
    core = lax.rem(index, 2)
    odd = lax.rem(g, 2) == 1
    own, one, two = own_ref[...], one_ref[...], two_ref[...]
    low = jnp.where(odd, one, two) * jnp.where(g > 0, 1.0, 0.0)
    high = jnp.where(odd, two, one) * jnp.where(g < 3, 1.0, 0.0)
    at_low = CZ * (low[3:4] + own[2:3]) * (low[1:2] - own[0:1])
    at_high = CZ * (high[2:3] + own[3:4]) * (high[0:1] - own[1:2])
    row = lax.broadcasted_iota(jnp.int32, (8, ROWS), 0)
    both = jnp.where(row == 0, at_low, jnp.where(row == 1, at_high, 0.0))
    fix_ref[...] = rows_to_lanes([(0, 0), (1, NZ - 1)], both, NZ).reshape(NX, NY, NZ)
    top = jnp.where(index == lax.axis_size("gx") - 1, CX, 0.0)
    inner = jnp.where(core == 0, NX - 1, 0)
    place = lax.rem(index, RING)
    inside = jnp.where(index >= RING, 1.0, 0.0)
    for which, out in ((core, keep_ref), (1 - core, send_ref)):
        ys = pl.ds(pl.multiple_of(which * HALF, HALF), HALF)
        r_h = rp_ref[0, ys] + fix_ref[0, ys]
        rr = rp_ref[1, ys] + fix_ref[1, ys]
        for j in range(1, NX - 1):
            rr_ref[j - 1, ys] = rr
            r_h = r_h + a_ref[j - 1, ys] * rr
            rr = (rp_ref[j + 1, ys] + fix_ref[j + 1, ys]) + m_ref[j - 1, ys] * rr
        out[0], out[2] = ew_ref[0, ys], ew_ref[2, ys]
        out[1] = ew_ref[1, ys] + top * k_ref[NX - 1, ys]
        out[3], out[4] = r_h, rr
        out[5] = k_ref[inner, ys]
        below, k = below_ref[ys], k_ref[0, ys]
        out[6] = jnp.where(place == 0, k, jnp.where(place == RING - 1, below * inside, CX * (below + k)))


def core_kernel(own_ref, got_ref, out_ref, parts_ref):
    index = lax.axis_index("gx")
    first = lax.rem(index, 2) == 0
    head = lax.rem(index, RING) < 2
    low = [jnp.where(first, own_ref[i], got_ref[i]) for i in range(7)]
    high = [jnp.where(first, got_ref[i], own_ref[i]) for i in range(7)]
    cut = jnp.where(head, 1.0, 0.0)
    near = jnp.where(head, 2.0 * low[2], low[2])
    e = [cut * low[0], (1.0 - cut) * low[0], low[1], high[0], high[1]]
    c = [jnp.where(head, near, low[6]), near, CX * (low[5] + high[5]), high[2]]
    r = [cut * low[3], (1.0 - cut) * low[3], low[4], high[3], high[4]]
    port, parts = reduce_chain(e, c, r)
    for i, v in enumerate(port):
        out_ref[i] = v
    out_ref[5] = jnp.where(head, low[6], high[6])
    for j, p in enumerate(parts):
        for i in range(3):
            parts_ref[3 * j + i] = p[i]


def ordered(me, refs, order, held):
    for i, ref in zip((0,) + order, refs):
        held[jnp.bitwise_xor(me, i)] = ref[...]


def chips_kernel(own_ref, one_ref, two_ref, three_ref, after_ref, also_ref, out_ref, parts_ref, held):
    del after_ref, also_ref
    me = lax.rem(lax.axis_index("gx") // 2, 4)
    ordered(me, (own_ref, one_ref, two_ref, three_ref), X_ORDER, held)
    blocks = [[held[b, i] for i in range(5)] for b in range(4)]
    e, c, r = join(blocks)
    below = CX * (held[0, 5] + held[3, 5])
    port, parts = reduce_chain([0.0] + e, [below] + c, [0.0] + r)
    for i, v in enumerate(port):
        out_ref[i] = v
    for j, p in enumerate(parts):
        for i in range(3):
            parts_ref[3 * j + i] = p[i]


def back_kernel(own_ref, one_ref, two_ref, three_ref, chips_ref, cores_ref, after_ref, keep_ref, send_ref, held, nodes):
    del after_ref
    index = lax.axis_index("gx")
    core, x, z = lax.rem(index, 2), lax.rem(index // 2, 4), index // 8
    ordered(z, (own_ref, one_ref, two_ref, three_ref), Z_ORDER, held)
    blocks = [[held[b, i] for i in range(5)] for b in range(4)]
    e, c, r = join(blocks)
    e[1] = e[1] + c[0]
    nodes[0] = jnp.zeros((HALF, NZ), F32)
    for i, v in enumerate(solve_chain(e[1:], c[1:], r[1:])):
        nodes[i + 1] = v
    first, last = nodes[z], nodes[z + 1]
    parts = [tuple(chips_ref[3 * j + i] for i in range(3)) for j in range(4)]
    for i, v in enumerate(expand_chain(first, last, parts)):
        nodes[i] = v
    first, last = nodes[x + 1], nodes[x + 2]
    parts = [tuple(cores_ref[3 * j + i] for i in range(3)) for j in range(3)]
    v = expand_chain(first, last, parts)
    v[1] = jnp.where(x == 0, v[0], v[1])
    even = core == 0
    keep_ref[0], keep_ref[1] = jnp.where(even, v[1], v[3]), jnp.where(even, v[2], v[4])
    send_ref[0], send_ref[1] = jnp.where(even, v[3], v[1]), jnp.where(even, v[4], v[2])


def y_major(ref, x, block):
    rows = ref.reshape(ROWS, NZ)
    for t in range(NY // 8):
        rows[pl.ds(t * 8 * NX + x, 8, stride=NX), :] = block[8 * t : 8 * t + 8]


def prepare_kernel(u_ref, k_ref, a_ref, m_ref, inv_ref, rr_ref, base_ref, g_ref, h_ref, my_ref, iy_ref):
    zero = jnp.zeros((NY, NZ), F32)
    y, g, h = zero, zero, zero + 1.0
    y_major(base_ref, NX - 1, -u_ref[NX - 1])
    y_major(g_ref, NX - 1, g)
    y_major(h_ref, NX - 1, h)
    for j in range(NX - 2, 0, -1):
        m = m_ref[j - 1]
        y = rr_ref[j - 1] * inv_ref[j - 1] + m * y
        g = a_ref[j - 1] + m * g
        h = m * h
        y_major(base_ref, j, y - u_ref[j])
        y_major(g_ref, j, g)
        y_major(h_ref, j, h)
    y_major(base_ref, 0, -u_ref[0])
    y_major(g_ref, 0, zero + 1.0)
    y_major(h_ref, 0, zero)
    k2 = k_ref.reshape(ROWS, NZ)
    at = lambda y: k2[pl.ds(y, NX, stride=NY), :]
    mid = HALF
    ends = []
    for start, step in ((0, 1), (NY - 1, -1)):
        k = at(start)
        ends.append([1.0 + CY * k, k, start, step])
    while any(e[2] != mid for e in ends):
        for e in ends:
            s, k, y, step = e
            if y == mid:
                continue
            k_next = at(y + step)
            c = CY * (k + k_next)
            inv = 1.0 / (s + c)
            m = c * inv
            my_ref[y], iy_ref[y] = m, inv
            e[0] = (0.0 if y + step == mid else 1.0) + m * s
            e[1], e[2] = k_next, y + step
    iy_ref[mid] = 1.0 / (1.0 + ends[0][0] + ends[1][0])
    my_ref[mid] = jnp.zeros((NX, NZ), F32)


LEVELS = 7
STEP = 32


def z_factors(k, keep):
    lane = lax.broadcasted_iota(jnp.int32, k.shape, 1)
    up = CZ * (k + pltpu.roll(k, NZ - 1, 1))
    low = pltpu.roll(up, 1, 1)
    top = up
    e = jnp.ones(k.shape, F32)
    for n in range(LEVELS):
        s = 1 << n
        inv = 1.0 / (e + low + up)
        has_low, has_up = lane >= s + 1, lane <= NZ - 2 - s
        low_in, up_in = jnp.where(has_low, low, 0.0), jnp.where(has_up, up, 0.0)
        keep(n, low_in, up_in, inv)
        share = e * inv
        e = e + low_in * pltpu.roll(share, s, 1) + up_in * pltpu.roll(share, NZ - s, 1)
        new_low = jnp.where(has_low, low * pltpu.roll(low * inv, s, 1), low)
        up = jnp.where(has_up, up * pltpu.roll(up * inv, NZ - s, 1), up)
        low = new_low
    inv = 1.0 / (e + low + up)
    first, last = lane == 0, lane == NZ - 1
    g = jnp.where(first, 1.0, jnp.where(last, 0.0, low * inv))
    h = jnp.where(first, 0.0, jnp.where(last, 1.0, up * inv))
    inv = jnp.where(first | last, 0.0, inv)
    return g, h, jnp.where(lane == NZ - 2, top * g, 0.0), inv


def z_ports_kernel(start, k_ref, u_ref, after_ref, uy_ref, g_ref, h_ref, port_ref, f_ref, t_ref):
    del after_ref
    k2, u2 = k_ref.reshape(ROWS, NZ), u_ref.reshape(ROWS, NZ)
    for y in range(HALF):
        uy_ref[y] = u2[pl.ds(start + y, NX, stride=NY), :]
    g2, h2 = g_ref.reshape(ROWS // 2, NZ), h_ref.reshape(ROWS // 2, NZ)

    def body(i, carry):
        y = start + i * STEP
        k = jnp.concatenate([k2[pl.ds(y + n, NX, stride=NY), :] for n in range(STEP)], axis=0)
        at = pl.ds(pl.multiple_of(i * (STEP * NX), NX * STEP), NX * STEP)

        def keep(n, *values):
            for j, v in enumerate(values):
                f_ref[3 * n + j, at, :] = v

        g, h, w, inv = z_factors(k, keep)
        f_ref[3 * LEVELS, at, :] = inv
        g2[at, :], h2[at, :] = g, h
        t_ref[0, at, :], t_ref[1, at, :] = k, w
        return carry

    lax.fori_loop(0, HALF // STEP, body, 0)
    port_ref[...] = (
        lanes_to_rows([(0, None)], g2[...])
        + lanes_to_rows([(1, None)], h2[...])
        + lanes_to_rows([(2, NZ - 2)], t_ref[1])
        + lanes_to_rows([(5, 0), (6, NZ - 1)], t_ref[0])
    )[:8]


def y_kernel(keep_ref, got_ref, base_ref, gx_ref, hx_ref, my_ref, iy_ref, g0_ref, g1_ref, h0_ref, h1_ref, p0_ref, p1_ref, v_ref, out_ref, b_ref, d_ref):
    core = lax.rem(lax.axis_index("gx"), 2)
    for i in range(2):
        b_ref[i, pl.ds(pl.multiple_of(core * HALF, HALF), HALF)] = keep_ref[i]
        b_ref[i, pl.ds(pl.multiple_of((1 - core) * HALF, HALF), HALF)] = got_ref[i]

    def at(y):
        first = jnp.broadcast_to(b_ref[0, y : y + 1, :], (NX, NZ))
        last = jnp.broadcast_to(b_ref[1, y : y + 1, :], (NX, NZ))
        return base_ref[y] + gx_ref[y] * first + hx_ref[y] * last

    mid = HALF
    low, high = at(0), at(NY - 1)
    for n in range(mid):
        y = n
        v_ref[y] = low * iy_ref[y]
        low = (at(y + 1) if y + 1 < mid else 0.0) + my_ref[y] * low
        y = NY - 1 - n
        if y > mid:
            v_ref[y] = high * iy_ref[y]
            high = (at(y - 1) if y - 1 > mid else 0.0) + my_ref[y] * high
    v = (at(mid) + low + high) * iy_ref[mid]
    low = high = v

    def emit(y, v):
        v_ref[y] = v
        g, h = (g0_ref, h0_ref) if y < HALF else (g1_ref, h1_ref)
        d_ref[0, y * NX : (y + 1) * NX, :] = g[y % HALF] * v
        d_ref[1, y * NX : (y + 1) * NX, :] = h[y % HALF] * v

    emit(mid, v)
    for n in range(1, mid + 1):
        y = mid - n
        low = v_ref[y] + my_ref[y] * low
        emit(y, low)
        y = mid + n
        if y < NY:
            high = v_ref[y] + my_ref[y] * high
            emit(y, high)
    out_ref[...] = (
        jnp.concatenate([p0_ref[...], p1_ref[...]], axis=1)
        + (lanes_to_rows([(3, None)], d_ref[0]) + lanes_to_rows([(4, None)], d_ref[1]))[:8]
    )


def z_local_kernel(f0_ref, f1_ref, u0_ref, u1_ref, v_ref, y_ref):
    v2, y2 = v_ref.reshape(ROWS, NZ), y_ref.reshape(ROWS, NZ)
    rows = STEP * NX

    for half, (f_ref, u_ref) in enumerate(((f0_ref, u0_ref), (f1_ref, u1_ref))):
        u2 = u_ref.reshape(ROWS // 2, NZ)

        def body(i, carry):
            at = pl.ds(pl.multiple_of(i * rows, rows), rows)
            full = pl.ds(pl.multiple_of(half * (ROWS // 2) + i * rows, rows), rows)
            r = v2[full, :]
            for n in range(LEVELS):
                s = 1 << n
                q = r * f_ref[3 * n + 2, at, :]
                r = (
                    r
                    + f_ref[3 * n, at, :] * pltpu.roll(q, s, 1)
                    + f_ref[3 * n + 1, at, :] * pltpu.roll(q, NZ - s, 1)
                )
            y2[full, :] = u2[at, :] + 2.0 * (r * f_ref[3 * LEVELS, at, :])
            return carry

        lax.fori_loop(0, HALF // STEP, body, 0)


CHUNK = 16


def final_kernel(own_ref, one_ref, two_ref, three_ref, y_ref, g0_ref, g1_ref, h0_ref, h1_ref, out_ref, held, b_ref, o_ref, *sems):
    me = lax.axis_index("gz")
    ordered(me, (own_ref, one_ref, two_ref, three_ref), L_ORDER, held)
    blocks = [[held[b, i : i + 1, :] for i in range(7)] for b in range(4)]
    e, c, r = [], [], []
    for i, b in enumerate(blocks):
        e += [b[0], b[1]]
        r += [b[3], b[4]]
        c.append(b[2])
        if i < 3:
            c.append(CZ * (b[6] + blocks[i + 1][5]))
    e[0] = e[0] + CZ * blocks[0][5]
    e[-1] = e[-1] + CZ * blocks[3][6]
    values = solve_chain(e, c, r)
    first, last = values[0], values[1]
    for b in range(1, 4):
        first = jnp.where(me == b, values[2 * b], first)
        last = jnp.where(me == b, values[2 * b + 1], last)
    row = lax.broadcasted_iota(jnp.int32, (8, ROWS), 0)
    both = jnp.where(row == 0, 2.0 * first, jnp.where(row == 1, 2.0 * last, 0.0))
    b_ref[...] = rows_to_lanes([(0, range(0, NZ)), (1, range(NZ, 2 * NZ))], both, 2 * NZ)
    o2 = o_ref.reshape(ROWS, NZ)
    copies = []
    for y in range(NY):
        ys = slice(y * NX, (y + 1) * NX)
        g, h = (g0_ref, h0_ref) if y < HALF else (g1_ref, h1_ref)
        o2[pl.ds(y, NX, stride=NY), :] = (
            y_ref[y] + g[y % HALF] * b_ref[ys, :NZ] + h[y % HALF] * b_ref[ys, NZ:]
        )
        if y % CHUNK == CHUNK - 1:
            part = pl.ds(y + 1 - CHUNK, CHUNK)
            copies.append(pltpu.make_async_copy(o_ref.at[:, part], out_ref.at[:, part], sems[y // CHUNK]))
            copies[-1].start()
    for copy in copies:
        copy.wait()


def swap(block, axis, mask):
    n = lax.axis_size(axis)
    return lax.ppermute(block, axis, [(i, i ^ mask) for i in range(n)])


def below_target(i, n):
    place = i % RING
    if place in (0, RING - 1):
        return (i + RING) % n
    return i + 1 if place % 2 else i - 1


def per_device(u, k, f):
    n = lax.axis_size("gx")
    u, k, f = (pltpu.with_memory_space_constraint(t, pltpu.HBM) for t in (u, k, f))
    u, k, f, edges, end = call(
        edges_kernel,
        [(NX, NY, NZ)] * 3 + [(8, ROWS), (NY, NZ)],
        u, k, f, sems=3, ins_in=pltpu.HBM, name="edges",
    )
    one, two = swap(edges, "gz", 1), swap(edges, "gz", 3)
    below = lax.ppermute(end, "gx", [(i, below_target(i, n)) for i in range(n)])
    rp, a, m, inv, ew = call(
        local_kernel,
        [(NX, NY, NZ), (NX - 2, NY, NZ), (NX - 2, NY, NZ), (NX - 2, NY, NZ), (3, NY, NZ)],
        u, k, f, name="local",
    )
    keep, send, rr = call(
        halo_kernel,
        [(7, HALF, NZ), (7, HALF, NZ), (NX - 2, NY, NZ)],
        edges, one, two, below, rp, a, m, ew, k, scratch=[(NX, NY, NZ)], name="halo",
    )
    got = swap(send, "gx", 1)
    chip, core_parts = call(core_kernel, [(6, HALF, NZ), (9, HALF, NZ)], keep, got, name="core")
    x_got = [swap(chip, "gx", 2 * i) for i in X_ORDER]
    base, gx, hx, my, iy = call(
        prepare_kernel, [(NY, NX, NZ)] * 5, u, k, a, m, inv, rr, name="prepare"
    )
    z_shapes = [(HALF, NX, NZ)] * 3 + [(8, ROWS // 2), (3 * LEVELS + 1, ROWS // 2, NZ)]
    u0, g0, h0, p0, f0 = call(
        functools.partial(z_ports_kernel, 0),
        z_shapes, k, u, chip, scratch=[(2, ROWS // 2, NZ)], name="z_ports",
    )
    group, chip_parts = call(
        chips_kernel,
        [(5, HALF, NZ), (12, HALF, NZ)],
        chip, *x_got, my, p0, scratch=[(4, 6, HALF, NZ)], name="chips",
    )
    z_got = [swap(group, "gx", 8 * i) for i in Z_ORDER]
    u1, g1, h1, p1, f1 = call(
        functools.partial(z_ports_kernel, HALF),
        z_shapes, k, u, group, scratch=[(2, ROWS // 2, NZ)], name="z_ports",
    )
    keep, send = call(
        back_kernel,
        [(2, HALF, NZ), (2, HALF, NZ)],
        group, *z_got, chip_parts, core_parts, p1,
        scratch=[(4, 5, HALF, NZ), (6, HALF, NZ)], name="back",
    )
    got = swap(send, "gx", 1)
    v, message = call(
        y_kernel,
        [(NY, NX, NZ), (8, ROWS)],
        keep, got, base, gx, hx, my, iy, g0, g1, h0, h1, p0, p1,
        scratch=[(2, NY, NZ), (2, ROWS, NZ)], name="y_solve",
    )
    l_got = [swap(message, "gz", i) for i in L_ORDER]
    yz, = call(z_local_kernel, [(NY, NX, NZ)], f0, f1, u0, u1, v, name="z_local")
    out, = call(
        final_kernel,
        [(NX, NY, NZ)],
        message, *l_got, yz, g0, g1, h0, h1,
        scratch=[(4, 8, ROWS), (ROWS, 2 * NZ), (NX, NY, NZ)], sems=NY // CHUNK,
        outs_in=pltpu.HBM, name="final",
    )
    return out


def solution(mesh):
    spec = P("gx", None, "gz")
    return jax.shard_map(
        per_device, mesh=mesh, in_specs=(spec, spec, spec), out_specs=spec, check_vma=False
    )
```

```python
import functools

import jax
import jax.numpy as jnp
from jax import lax
from jax.experimental import pallas as pl
from jax.experimental.pallas import tpu as pltpu
from jax.sharding import PartitionSpec as P

NX, NY, NZ = 8, 64, 128
ROWS = NX * NY
HALF = NY // 2
RING = 8
CX = 0.25 * 16.0 * NX * NX
CY = 0.25 * 2.0
CZ = 0.25 * 0.5 * NZ * NZ
F32 = jnp.float32
VMEM_LIMIT = 24 * 1024 * 1024
BF16 = jnp.bfloat16
X_ORDER, Z_ORDER, L_ORDER = ((2, 3), (3, 2), (1, 1)), ((2, 3), (3, 2), (1, 1)), ((3, 3), (2, 2), (1, 1))
X_FLIP, Z_FLIP = 2, 2


def flips(distance, bits):
    both = distance & bits
    return (both ^ (both >> 1)) & 1


def half_of(index):
    return (index & 1) ^ flips((index >> 1) & 3, X_FLIP) ^ flips(index >> 3, Z_FLIP)


def call(kernel, outs, *args, scratch=(), sems=0, ins_in=pltpu.VMEM, outs_in=pltpu.VMEM, flops=0, name=None):
    shapes = [jax.ShapeDtypeStruct(s, F32) for s in outs]
    nbytes = sum(4 * a.size for a in args) + sum(4 * s.size for s in shapes)
    return pl.pallas_call(
        kernel,
        out_shape=shapes,
        in_specs=[pl.BlockSpec(memory_space=ins_in) for _ in args],
        out_specs=[pl.BlockSpec(memory_space=outs_in) for _ in outs],
        scratch_shapes=[pltpu.VMEM(s, F32) for s in scratch]
        + [pltpu.SemaphoreType.DMA] * sems,
        compiler_params=pltpu.CompilerParams(vmem_limit_bytes=VMEM_LIMIT),
        cost_estimate=pl.CostEstimate(flops=flops, bytes_accessed=nbytes, transcendentals=0),
        name=name,
    )(*args)


def pieces(x):
    high = x.astype(BF16).astype(F32)
    rest = x - high
    middle = rest.astype(BF16).astype(F32)
    return high, middle, rest - middle


def lanes_to_rows(entries, block):
    high, middle, low = (p.astype(BF16) for p in pieces(block))
    select = selector(entries, 16, NZ).astype(BF16)
    dims = (((1,), (1,)), ((), ()))
    return lax.dot_general(
        jnp.concatenate([select, select], axis=1),
        jnp.concatenate([high, middle], axis=1),
        dims,
        preferred_element_type=F32,
    ) + lax.dot_general(select, low, dims, preferred_element_type=F32)


def rows_to_lanes(entries, rows, lanes):
    both = jnp.concatenate(pieces(rows) + (jnp.zeros_like(rows),), axis=0).astype(BF16)
    select = selector([(r + 8 * i, l) for i in range(3) for r, l in entries], 32, lanes)
    return lax.dot_general(
        both, select.astype(BF16), (((0,), (0,)), ((), ())), preferred_element_type=F32
    )


def selector(entries, rows, lanes):
    row = lax.broadcasted_iota(jnp.int32, (rows, lanes), 0)
    lane = lax.broadcasted_iota(jnp.int32, (rows, lanes), 1)
    hit = None
    for r, l in entries:
        one = row == r
        if isinstance(l, range):
            one = one & (lane >= l.start) & (lane < l.stop)
        elif l is not None:
            one = one & (lane == l)
        hit = one if hit is None else (hit | one)
    return jnp.where(hit, 1.0, 0.0).astype(F32)


def reduce_chain(e, c, r):
    n = len(e)
    e_h, r_h = e[0], r[0]
    s, w, rr = e[1], c[0], r[1]
    parts = []
    for j in range(1, n - 1):
        inv = 1.0 / (s + w + c[j])
        a, m = w * inv, c[j] * inv
        parts.append((a, m, rr * inv))
        e_h = e_h + a * s
        r_h = r_h + a * rr
        s = e[j + 1] + m * s
        rr = r[j + 1] + m * rr
        w = m * w
    return (e_h, s, w, r_h, rr), parts


def expand_chain(first, last, parts):
    values = [last]
    for a, m, q in reversed(parts):
        values.append(q + a * first + m * values[-1])
    values.append(first)
    return values[::-1]


def solve_chain(e, c, r):
    n = len(e)
    mid = n // 2
    low, high = [], []
    s, rr = e[0], r[0]
    t, tt = e[n - 1], r[n - 1]
    for j in range(mid):
        inv = 1.0 / (s + c[j])
        m = c[j] * inv
        low.append((m, rr * inv))
        s, rr = e[j + 1] + m * s, r[j + 1] + m * rr
        i = n - 1 - j
        if i > mid:
            inv = 1.0 / (t + c[i - 1])
            m = c[i - 1] * inv
            high.append((m, tt * inv))
            t, tt = m * t, m * tt
            if i - 1 > mid:
                t, tt = e[i - 1] + t, r[i - 1] + tt
    values = [None] * n
    values[mid] = (rr + tt) / (s + t)
    for j in range(mid - 1, -1, -1):
        m, q = low[j]
        values[j] = q + m * values[j + 1]
    for i in range(mid + 1, n):
        m, q = high[n - 1 - i]
        values[i] = q + m * values[i - 1]
    return values


def join(blocks):
    e = [blocks[0][0]]
    r = [blocks[0][3]]
    for i, b in enumerate(blocks):
        e.append(b[1] + blocks[i + 1][0] if i + 1 < len(blocks) else b[1])
        r.append(b[4] + blocks[i + 1][3] if i + 1 < len(blocks) else b[4])
    return e, [b[2] for b in blocks], r


def edges_kernel(u_hbm, k_hbm, f_hbm, u_ref, k_ref, f_ref, out_ref, end_ref, *sems):
    pairs = ((k_hbm, k_ref), (u_hbm, u_ref), (f_hbm, f_ref))
    copies = [pltpu.make_async_copy(a, b, sem) for (a, b), sem in zip(pairs, sems)]
    for copy in copies:
        copy.start()
    lane = lax.broadcasted_iota(jnp.int32, (ROWS, NZ), 1)
    copies[0].wait()
    k = pltpu.roll(k_ref[...].reshape(ROWS, NZ), 2, 1)
    copies[1].wait()
    both = jnp.where((lane == 1) | (lane == 2), k, u_ref[...].reshape(ROWS, NZ))
    out_ref[...] = lanes_to_rows([(0, 0), (1, NZ - 1), (2, 2), (3, 1)], both)[:8]
    index = lax.axis_index("gx")
    end_ref[...] = k_ref[jnp.where(lax.rem(index, 2) == 1, NX - 1, 0)]
    copies[2].wait()


def local_kernel(u_ref, k_ref, f_ref, rp_ref, a_ref, m_ref, inv_ref, ew_ref):
    row = lax.broadcasted_iota(jnp.int32, (NY, NZ), 0)
    lane = lax.broadcasted_iota(jnp.int32, (NY, NZ), 1)
    for x in range(NX):
        u, k = u_ref[x], k_ref[x]
        flux_y = (CY * (k + pltpu.roll(k, NY - 1, 0))) * (pltpu.roll(u, NY - 1, 0) - u)
        flux_y = jnp.where(row == NY - 1, -(CY * k) * u, flux_y)
        low_y = jnp.where(row == 0, (CY * k) * u, pltpu.roll(flux_y, 1, 0))
        flux_z = (CZ * (k + pltpu.roll(k, NZ - 1, 1))) * (pltpu.roll(u, NZ - 1, 1) - u)
        flux_z = jnp.where(lane == NZ - 1, 0.0, flux_z)
        low_z = pltpu.roll(flux_z, 1, 1)
        rp_ref[x] = u + (flux_y - low_y) + (flux_z - low_z) + 0.5 * f_ref[x]
    s = jnp.ones((NY, NZ), F32)
    e_h = s
    w = CX * (k_ref[0] + k_ref[1])
    for j in range(1, NX - 1):
        c = CX * (k_ref[j] + k_ref[j + 1])
        inv = 1.0 / (s + w + c)
        a, m = w * inv, c * inv
        inv_ref[j - 1], a_ref[j - 1], m_ref[j - 1] = inv, a, m
        e_h = e_h + a * s
        s = 1.0 + m * s
        w = m * w
    ew_ref[0], ew_ref[1], ew_ref[2] = e_h, s, w


def halo_kernel(own_ref, one_ref, two_ref, below_ref, rp_ref, a_ref, m_ref, ew_ref, k_ref, keep_ref, send_ref, rr_ref, fix_ref):
    g = lax.axis_index("gz")
    index = lax.axis_index("gx")
    core = lax.rem(index, 2)
    odd = lax.rem(g, 2) == 1
    own, one, two = own_ref[...], one_ref[...], two_ref[...]
    low = jnp.where(odd, one, two) * jnp.where(g > 0, 1.0, 0.0)
    high = jnp.where(odd, two, one) * jnp.where(g < 3, 1.0, 0.0)
    at_low = CZ * (low[3:4] + own[2:3]) * (low[1:2] - own[0:1])
    at_high = CZ * (high[2:3] + own[3:4]) * (high[0:1] - own[1:2])
    row = lax.broadcasted_iota(jnp.int32, (8, ROWS), 0)
    both = jnp.where(row == 0, at_low, jnp.where(row == 1, at_high, 0.0))
    fix_ref[...] = rows_to_lanes([(0, 0), (1, NZ - 1)], both, NZ).reshape(NX, NY, NZ)
    top = jnp.where(index == lax.axis_size("gx") - 1, CX, 0.0)
    inner = jnp.where(core == 0, NX - 1, 0)
    place = lax.rem(index, RING)
    inside = jnp.where(index >= RING, 1.0, 0.0)
    half = half_of(index)
    for which, out in ((half, keep_ref), (1 - half, send_ref)):
        ys = pl.ds(pl.multiple_of(which * HALF, HALF), HALF)
        r_h = rp_ref[0, ys] + fix_ref[0, ys]
        rr = rp_ref[1, ys] + fix_ref[1, ys]
        for j in range(1, NX - 1):
            rr_ref[j - 1, ys] = rr
            r_h = r_h + a_ref[j - 1, ys] * rr
            rr = (rp_ref[j + 1, ys] + fix_ref[j + 1, ys]) + m_ref[j - 1, ys] * rr
        out[0], out[2] = ew_ref[0, ys], ew_ref[2, ys]
        out[1] = ew_ref[1, ys] + top * k_ref[NX - 1, ys]
        out[3], out[4] = r_h, rr
        out[5] = k_ref[inner, ys]
        below, k = below_ref[ys], k_ref[0, ys]
        out[6] = jnp.where(place == 0, k, jnp.where(place == RING - 1, below * inside, CX * (below + k)))


def core_kernel(own_ref, got_ref, out_ref, parts_ref):
    index = lax.axis_index("gx")
    first = lax.rem(index, 2) == 0
    head = lax.rem(index, RING) < 2
    low = [jnp.where(first, own_ref[i], got_ref[i]) for i in range(7)]
    high = [jnp.where(first, got_ref[i], own_ref[i]) for i in range(7)]
    cut = jnp.where(head, 1.0, 0.0)
    near = jnp.where(head, 2.0 * low[2], low[2])
    e = [cut * low[0], (1.0 - cut) * low[0], low[1], high[0], high[1]]
    c = [jnp.where(head, near, low[6]), near, CX * (low[5] + high[5]), high[2]]
    r = [cut * low[3], (1.0 - cut) * low[3], low[4], high[3], high[4]]
    port, parts = reduce_chain(e, c, r)
    for i, v in enumerate(port):
        out_ref[i] = v
    out_ref[5] = jnp.where(head, low[6], high[6])
    for j, p in enumerate(parts):
        for i in range(3):
            parts_ref[3 * j + i] = p[i]


def ordered(me, refs, order, held):
    half = half_of(lax.axis_index("gx"))
    for pair, ref in zip(((0, 0),) + order, refs):
        held[jnp.bitwise_xor(me, jnp.where(half == 0, pair[0], pair[1]))] = ref[...]


def chips_kernel(own_ref, one_ref, two_ref, three_ref, after_ref, also_ref, out_ref, parts_ref, held):
    del after_ref, also_ref
    me = lax.rem(lax.axis_index("gx") // 2, 4)
    ordered(me, (own_ref, one_ref, two_ref, three_ref), X_ORDER, held)
    blocks = [[held[b, i] for i in range(5)] for b in range(4)]
    e, c, r = join(blocks)
    below = CX * (held[0, 5] + held[3, 5])
    port, parts = reduce_chain([0.0] + e, [below] + c, [0.0] + r)
    for i, v in enumerate(port):
        out_ref[i] = v
    for j, p in enumerate(parts):
        for i in range(3):
            parts_ref[3 * j + i] = p[i]


def back_kernel(own_ref, one_ref, two_ref, three_ref, chips_ref, cores_ref, after_ref, keep_ref, send_ref, held, nodes):
    del after_ref
    index = lax.axis_index("gx")
    core, x, z = lax.rem(index, 2), lax.rem(index // 2, 4), index // 8
    ordered(z, (own_ref, one_ref, two_ref, three_ref), Z_ORDER, held)
    blocks = [[held[b, i] for i in range(5)] for b in range(4)]
    e, c, r = join(blocks)
    e[1] = e[1] + c[0]
    nodes[0] = jnp.zeros((HALF, NZ), F32)
    for i, v in enumerate(solve_chain(e[1:], c[1:], r[1:])):
        nodes[i + 1] = v
    first, last = nodes[z], nodes[z + 1]
    parts = [tuple(chips_ref[3 * j + i] for i in range(3)) for j in range(4)]
    for i, v in enumerate(expand_chain(first, last, parts)):
        nodes[i] = v
    first, last = nodes[x + 1], nodes[x + 2]
    parts = [tuple(cores_ref[3 * j + i] for i in range(3)) for j in range(3)]
    v = expand_chain(first, last, parts)
    v[1] = jnp.where(x == 0, v[0], v[1])
    even = core == 0
    keep_ref[0], keep_ref[1] = jnp.where(even, v[1], v[3]), jnp.where(even, v[2], v[4])
    send_ref[0], send_ref[1] = jnp.where(even, v[3], v[1]), jnp.where(even, v[4], v[2])


def y_major(ref, x, block):
    rows = ref.reshape(ROWS, NZ)
    for t in range(NY // 8):
        rows[pl.ds(t * 8 * NX + x, 8, stride=NX), :] = block[8 * t : 8 * t + 8]


def prepare_kernel(u_ref, k_ref, a_ref, m_ref, inv_ref, rr_ref, base_ref, g_ref, h_ref, my_ref, iy_ref):
    zero = jnp.zeros((NY, NZ), F32)
    y, g, h = zero, zero, zero + 1.0
    y_major(base_ref, NX - 1, -u_ref[NX - 1])
    y_major(g_ref, NX - 1, g)
    y_major(h_ref, NX - 1, h)
    for j in range(NX - 2, 0, -1):
        m = m_ref[j - 1]
        y = rr_ref[j - 1] * inv_ref[j - 1] + m * y
        g = a_ref[j - 1] + m * g
        h = m * h
        y_major(base_ref, j, y - u_ref[j])
        y_major(g_ref, j, g)
        y_major(h_ref, j, h)
    y_major(base_ref, 0, -u_ref[0])
    y_major(g_ref, 0, zero + 1.0)
    y_major(h_ref, 0, zero)
    k2 = k_ref.reshape(ROWS, NZ)
    at = lambda y: k2[pl.ds(y, NX, stride=NY), :]
    mid = HALF
    ends = []
    for start, step in ((0, 1), (NY - 1, -1)):
        k = at(start)
        ends.append([1.0 + CY * k, k, start, step])
    while any(e[2] != mid for e in ends):
        for e in ends:
            s, k, y, step = e
            if y == mid:
                continue
            k_next = at(y + step)
            c = CY * (k + k_next)
            inv = 1.0 / (s + c)
            m = c * inv
            my_ref[y], iy_ref[y] = m, inv
            e[0] = (0.0 if y + step == mid else 1.0) + m * s
            e[1], e[2] = k_next, y + step
    iy_ref[mid] = 1.0 / (1.0 + ends[0][0] + ends[1][0])
    my_ref[mid] = jnp.zeros((NX, NZ), F32)


LEVELS = 7
STEP = 32


def z_factors(k, keep):
    lane = lax.broadcasted_iota(jnp.int32, k.shape, 1)
    up = CZ * (k + pltpu.roll(k, NZ - 1, 1))
    low = pltpu.roll(up, 1, 1)
    top = up
    e = jnp.ones(k.shape, F32)
    for n in range(LEVELS):
        s = 1 << n
        inv = 1.0 / (e + low + up)
        has_low, has_up = lane >= s + 1, lane <= NZ - 2 - s
        low_in, up_in = jnp.where(has_low, low, 0.0), jnp.where(has_up, up, 0.0)
        keep(n, low_in, up_in, inv)
        share = e * inv
        e = e + low_in * pltpu.roll(share, s, 1) + up_in * pltpu.roll(share, NZ - s, 1)
        new_low = jnp.where(has_low, low * pltpu.roll(low * inv, s, 1), low)
        up = jnp.where(has_up, up * pltpu.roll(up * inv, NZ - s, 1), up)
        low = new_low
    inv = 1.0 / (e + low + up)
    first, last = lane == 0, lane == NZ - 1
    g = jnp.where(first, 1.0, jnp.where(last, 0.0, low * inv))
    h = jnp.where(first, 0.0, jnp.where(last, 1.0, up * inv))
    inv = jnp.where(first | last, 0.0, inv)
    return g, h, jnp.where(lane == NZ - 2, top * g, 0.0), inv


def z_ports_kernel(start, k_ref, u_ref, after_ref, uy_ref, g_ref, h_ref, port_ref, f_ref, t_ref):
    del after_ref
    k2, u2 = k_ref.reshape(ROWS, NZ), u_ref.reshape(ROWS, NZ)
    for y in range(HALF):
        uy_ref[y] = u2[pl.ds(start + y, NX, stride=NY), :]
    g2, h2 = g_ref.reshape(ROWS // 2, NZ), h_ref.reshape(ROWS // 2, NZ)

    def body(i, carry):
        y = start + i * STEP
        k = jnp.concatenate([k2[pl.ds(y + n, NX, stride=NY), :] for n in range(STEP)], axis=0)
        at = pl.ds(pl.multiple_of(i * (STEP * NX), NX * STEP), NX * STEP)

        def keep(n, *values):
            for j, v in enumerate(values):
                f_ref[3 * n + j, at, :] = v

        g, h, w, inv = z_factors(k, keep)
        f_ref[3 * LEVELS, at, :] = inv
        g2[at, :], h2[at, :] = g, h
        t_ref[0, at, :], t_ref[1, at, :] = k, w
        return carry

    lax.fori_loop(0, HALF // STEP, body, 0)
    port_ref[...] = (
        lanes_to_rows([(0, None)], g2[...])
        + lanes_to_rows([(1, None)], h2[...])
        + lanes_to_rows([(2, NZ - 2)], t_ref[1])
        + lanes_to_rows([(5, 0), (6, NZ - 1)], t_ref[0])
    )[:8]


def y_kernel(keep_ref, got_ref, base_ref, gx_ref, hx_ref, my_ref, iy_ref, g0_ref, g1_ref, h0_ref, h1_ref, p0_ref, p1_ref, v_ref, out_ref, b_ref, d_ref):
    half = half_of(lax.axis_index("gx"))
    for i in range(2):
        b_ref[i, pl.ds(pl.multiple_of(half * HALF, HALF), HALF)] = keep_ref[i]
        b_ref[i, pl.ds(pl.multiple_of((1 - half) * HALF, HALF), HALF)] = got_ref[i]

    def at(y):
        first = jnp.broadcast_to(b_ref[0, y : y + 1, :], (NX, NZ))
        last = jnp.broadcast_to(b_ref[1, y : y + 1, :], (NX, NZ))
        return base_ref[y] + gx_ref[y] * first + hx_ref[y] * last

    mid = HALF
    low, high = at(0), at(NY - 1)
    for n in range(mid):
        y = n
        v_ref[y] = low * iy_ref[y]
        low = (at(y + 1) if y + 1 < mid else 0.0) + my_ref[y] * low
        y = NY - 1 - n
        if y > mid:
            v_ref[y] = high * iy_ref[y]
            high = (at(y - 1) if y - 1 > mid else 0.0) + my_ref[y] * high
    v = (at(mid) + low + high) * iy_ref[mid]
    low = high = v

    def emit(y, v):
        v_ref[y] = v
        g, h = (g0_ref, h0_ref) if y < HALF else (g1_ref, h1_ref)
        d_ref[0, y * NX : (y + 1) * NX, :] = g[y % HALF] * v
        d_ref[1, y * NX : (y + 1) * NX, :] = h[y % HALF] * v

    emit(mid, v)
    for n in range(1, mid + 1):
        y = mid - n
        low = v_ref[y] + my_ref[y] * low
        emit(y, low)
        y = mid + n
        if y < NY:
            high = v_ref[y] + my_ref[y] * high
            emit(y, high)
    out_ref[...] = (
        jnp.concatenate([p0_ref[...], p1_ref[...]], axis=1)
        + (lanes_to_rows([(3, None)], d_ref[0]) + lanes_to_rows([(4, None)], d_ref[1]))[:8]
    )


def z_local_kernel(f0_ref, f1_ref, u0_ref, u1_ref, v_ref, y_ref):
    v2, y2 = v_ref.reshape(ROWS, NZ), y_ref.reshape(ROWS, NZ)
    rows = STEP * NX

    for half, (f_ref, u_ref) in enumerate(((f0_ref, u0_ref), (f1_ref, u1_ref))):
        u2 = u_ref.reshape(ROWS // 2, NZ)

        def body(i, carry):
            at = pl.ds(pl.multiple_of(i * rows, rows), rows)
            full = pl.ds(pl.multiple_of(half * (ROWS // 2) + i * rows, rows), rows)
            r = v2[full, :]
            for n in range(LEVELS):
                s = 1 << n
                q = r * f_ref[3 * n + 2, at, :]
                r = (
                    r
                    + f_ref[3 * n, at, :] * pltpu.roll(q, s, 1)
                    + f_ref[3 * n + 1, at, :] * pltpu.roll(q, NZ - s, 1)
                )
            y2[full, :] = u2[at, :] + 2.0 * (r * f_ref[3 * LEVELS, at, :])
            return carry

        lax.fori_loop(0, HALF // STEP, body, 0)


CHUNK = 16


def final_kernel(own_ref, one_ref, two_ref, three_ref, y_ref, g0_ref, g1_ref, h0_ref, h1_ref, out_ref, held, b_ref, o_ref, *sems):
    me = lax.axis_index("gz")
    ordered(me, (own_ref, one_ref, two_ref, three_ref), L_ORDER, held)
    blocks = [[held[b, i : i + 1, :] for i in range(7)] for b in range(4)]
    e, c, r = [], [], []
    for i, b in enumerate(blocks):
        e += [b[0], b[1]]
        r += [b[3], b[4]]
        c.append(b[2])
        if i < 3:
            c.append(CZ * (b[6] + blocks[i + 1][5]))
    e[0] = e[0] + CZ * blocks[0][5]
    e[-1] = e[-1] + CZ * blocks[3][6]
    values = solve_chain(e, c, r)
    first, last = values[0], values[1]
    for b in range(1, 4):
        first = jnp.where(me == b, values[2 * b], first)
        last = jnp.where(me == b, values[2 * b + 1], last)
    row = lax.broadcasted_iota(jnp.int32, (8, ROWS), 0)
    both = jnp.where(row == 0, 2.0 * first, jnp.where(row == 1, 2.0 * last, 0.0))
    b_ref[...] = rows_to_lanes([(0, range(0, NZ)), (1, range(NZ, 2 * NZ))], both, 2 * NZ)
    o2 = o_ref.reshape(ROWS, NZ)
    copies = []
    for y in range(NY):
        ys = slice(y * NX, (y + 1) * NX)
        g, h = (g0_ref, h0_ref) if y < HALF else (g1_ref, h1_ref)
        o2[pl.ds(y, NX, stride=NY), :] = (
            y_ref[y] + g[y % HALF] * b_ref[ys, :NZ] + h[y % HALF] * b_ref[ys, NZ:]
        )
        if y % CHUNK == CHUNK - 1:
            part = pl.ds(y + 1 - CHUNK, CHUNK)
            copies.append(pltpu.make_async_copy(o_ref.at[:, part], out_ref.at[:, part], sems[y // CHUNK]))
            copies[-1].start()
    for copy in copies:
        copy.wait()


def swap(block, axis, mask):
    n = lax.axis_size(axis)
    return lax.ppermute(block, axis, [(i, i ^ mask) for i in range(n)])


def gather(block, unit, order, bits):
    got = []
    for pair in order:
        route = []
        for i in range(lax.axis_size("gx")):
            distance = pair[half_of(i)]
            route.append((i, i ^ (unit * distance) ^ flips(distance, bits)))
        got.append(lax.ppermute(block, "gx", route))
    return got


def below_target(i, n):
    place = i % RING
    if place == 0:
        return i ^ RING
    if place == RING - 1:
        return (i + RING) % n
    return i + 1 if place % 2 else i - 1


def per_device(u, k, f):
    n = lax.axis_size("gx")
    u, k, f = (pltpu.with_memory_space_constraint(t, pltpu.HBM) for t in (u, k, f))
    u, k, f, edges, end = call(
        edges_kernel,
        [(NX, NY, NZ)] * 3 + [(8, ROWS), (NY, NZ)],
        u, k, f, sems=3, ins_in=pltpu.HBM, name="edges",
    )
    nz = lax.axis_size("gz")
    inner = [
        (i * nz + j, (i ^ 1) * nz + j if j in (0, nz - 1) else i * nz + (j ^ 3))
        for i in range(n)
        for j in range(nz)
    ]
    one, two = swap(edges, "gz", 1), lax.ppermute(edges, ("gx", "gz"), inner)
    below = lax.ppermute(end, "gx", [(i, below_target(i, n)) for i in range(n)])
    rp, a, m, inv, ew = call(
        local_kernel,
        [(NX, NY, NZ), (NX - 2, NY, NZ), (NX - 2, NY, NZ), (NX - 2, NY, NZ), (3, NY, NZ)],
        u, k, f, name="local",
    )
    keep, send, rr = call(
        halo_kernel,
        [(7, HALF, NZ), (7, HALF, NZ), (NX - 2, NY, NZ)],
        edges, one, two, below, rp, a, m, ew, k, scratch=[(NX, NY, NZ)], name="halo",
    )
    got = swap(send, "gx", 1)
    chip, core_parts = call(core_kernel, [(6, HALF, NZ), (9, HALF, NZ)], keep, got, name="core")
    x_got = gather(chip, 2, X_ORDER, X_FLIP)
    base, gx, hx, my, iy = call(
        prepare_kernel, [(NY, NX, NZ)] * 5, u, k, a, m, inv, rr, name="prepare"
    )
    z_shapes = [(HALF, NX, NZ)] * 3 + [(8, ROWS // 2), (3 * LEVELS + 1, ROWS // 2, NZ)]
    u0, g0, h0, p0, f0 = call(
        functools.partial(z_ports_kernel, 0),
        z_shapes, k, u, chip, scratch=[(2, ROWS // 2, NZ)], name="z_ports",
    )
    group, chip_parts = call(
        chips_kernel,
        [(5, HALF, NZ), (12, HALF, NZ)],
        chip, *x_got, my, p0, scratch=[(4, 6, HALF, NZ)], name="chips",
    )
    z_got = gather(group, 8, Z_ORDER, Z_FLIP)
    u1, g1, h1, p1, f1 = call(
        functools.partial(z_ports_kernel, HALF),
        z_shapes, k, u, group, scratch=[(2, ROWS // 2, NZ)], name="z_ports",
    )
    keep, send = call(
        back_kernel,
        [(2, HALF, NZ), (2, HALF, NZ)],
        group, *z_got, chip_parts, core_parts, p1,
        scratch=[(4, 5, HALF, NZ), (6, HALF, NZ)], name="back",
    )
    got = swap(send, "gx", 1)
    v, message = call(
        y_kernel,
        [(NY, NX, NZ), (8, ROWS)],
        keep, got, base, gx, hx, my, iy, g0, g1, h0, h1, p0, p1,
        scratch=[(2, NY, NZ), (2, ROWS, NZ)], name="y_solve",
    )
    l_got = [swap(message, "gz", i) for i, _ in L_ORDER]
    yz, = call(z_local_kernel, [(NY, NX, NZ)], f0, f1, u0, u1, v, name="z_local")
    out, = call(
        final_kernel,
        [(NX, NY, NZ)],
        message, *l_got, yz, g0, g1, h0, h1,
        scratch=[(4, 8, ROWS), (ROWS, 2 * NZ), (NX, NY, NZ)], sems=NY // CHUNK,
        outs_in=pltpu.HBM, name="final",
    )
    return out


def solution(mesh):
    spec = P("gx", None, "gz")
    return jax.shard_map(
        per_device, mesh=mesh, in_specs=(spec, spec, spec), out_specs=spec, check_vma=False
    )
```

```python
import functools

import jax
import jax.numpy as jnp
from jax import lax
from jax.experimental import pallas as pl
from jax.experimental.pallas import tpu as pltpu
from jax.sharding import PartitionSpec as P

NX, NY, NZ = 8, 64, 128
ROWS = NX * NY
HALF = NY // 2
RING = 8
CX = 0.25 * 16.0 * NX * NX
CY = 0.25 * 2.0
CZ = 0.25 * 0.5 * NZ * NZ
F32 = jnp.float32
VMEM_LIMIT = 24 * 1024 * 1024
BF16 = jnp.bfloat16
X_ORDER, Z_ORDER, L_ORDER = ((2, 3), (3, 2), (1, 1)), ((3, 3), (2, 2), (1, 1)), ((3, 3), (2, 2), (1, 1))
X_FLIP, Z_FLIP = 2, 2


def flips(distance, bits):
    both = distance & bits
    return (both ^ (both >> 1)) & 1


def half_of(index):
    return (index & 1) ^ flips((index >> 1) & 3, X_FLIP) ^ flips(index >> 3, Z_FLIP)


def call(kernel, outs, *args, scratch=(), sems=0, ins_in=pltpu.VMEM, outs_in=pltpu.VMEM, flops=0, name=None):
    shapes = [jax.ShapeDtypeStruct(s, F32) for s in outs]
    nbytes = sum(4 * a.size for a in args) + sum(4 * s.size for s in shapes)
    return pl.pallas_call(
        kernel,
        out_shape=shapes,
        in_specs=[pl.BlockSpec(memory_space=ins_in) for _ in args],
        out_specs=[pl.BlockSpec(memory_space=outs_in) for _ in outs],
        scratch_shapes=[pltpu.VMEM(s, F32) for s in scratch]
        + [pltpu.SemaphoreType.DMA] * sems,
        compiler_params=pltpu.CompilerParams(vmem_limit_bytes=VMEM_LIMIT),
        cost_estimate=pl.CostEstimate(flops=flops, bytes_accessed=nbytes, transcendentals=0),
        name=name,
    )(*args)


def pieces(x):
    high = x.astype(BF16).astype(F32)
    rest = x - high
    middle = rest.astype(BF16).astype(F32)
    return high, middle, rest - middle


def lanes_to_rows(entries, block):
    high, middle, low = (p.astype(BF16) for p in pieces(block))
    select = selector(entries, 16, NZ).astype(BF16)
    dims = (((1,), (1,)), ((), ()))
    return lax.dot_general(
        jnp.concatenate([select, select], axis=1),
        jnp.concatenate([high, middle], axis=1),
        dims,
        preferred_element_type=F32,
    ) + lax.dot_general(select, low, dims, preferred_element_type=F32)


def rows_to_lanes(entries, rows, lanes):
    both = jnp.concatenate(pieces(rows) + (jnp.zeros_like(rows),), axis=0).astype(BF16)
    select = selector([(r + 8 * i, l) for i in range(3) for r, l in entries], 32, lanes)
    return lax.dot_general(
        both, select.astype(BF16), (((0,), (0,)), ((), ())), preferred_element_type=F32
    )


def selector(entries, rows, lanes):
    row = lax.broadcasted_iota(jnp.int32, (rows, lanes), 0)
    lane = lax.broadcasted_iota(jnp.int32, (rows, lanes), 1)
    hit = None
    for r, l in entries:
        one = row == r
        if isinstance(l, range):
            one = one & (lane >= l.start) & (lane < l.stop)
        elif l is not None:
            one = one & (lane == l)
        hit = one if hit is None else (hit | one)
    return jnp.where(hit, 1.0, 0.0).astype(F32)


def reduce_chain(e, c, r):
    n = len(e)
    e_h, r_h = e[0], r[0]
    s, w, rr = e[1], c[0], r[1]
    parts = []
    for j in range(1, n - 1):
        inv = 1.0 / (s + w + c[j])
        a, m = w * inv, c[j] * inv
        parts.append((a, m, rr * inv))
        e_h = e_h + a * s
        r_h = r_h + a * rr
        s = e[j + 1] + m * s
        rr = r[j + 1] + m * rr
        w = m * w
    return (e_h, s, w, r_h, rr), parts


def expand_chain(first, last, parts):
    values = [last]
    for a, m, q in reversed(parts):
        values.append(q + a * first + m * values[-1])
    values.append(first)
    return values[::-1]


def solve_chain(e, c, r):
    n = len(e)
    mid = n // 2
    low, high = [], []
    s, rr = e[0], r[0]
    t, tt = e[n - 1], r[n - 1]
    for j in range(mid):
        inv = 1.0 / (s + c[j])
        m = c[j] * inv
        low.append((m, rr * inv))
        s, rr = e[j + 1] + m * s, r[j + 1] + m * rr
        i = n - 1 - j
        if i > mid:
            inv = 1.0 / (t + c[i - 1])
            m = c[i - 1] * inv
            high.append((m, tt * inv))
            t, tt = m * t, m * tt
            if i - 1 > mid:
                t, tt = e[i - 1] + t, r[i - 1] + tt
    values = [None] * n
    values[mid] = (rr + tt) / (s + t)
    for j in range(mid - 1, -1, -1):
        m, q = low[j]
        values[j] = q + m * values[j + 1]
    for i in range(mid + 1, n):
        m, q = high[n - 1 - i]
        values[i] = q + m * values[i - 1]
    return values


def join(blocks):
    e = [blocks[0][0]]
    r = [blocks[0][3]]
    for i, b in enumerate(blocks):
        e.append(b[1] + blocks[i + 1][0] if i + 1 < len(blocks) else b[1])
        r.append(b[4] + blocks[i + 1][3] if i + 1 < len(blocks) else b[4])
    return e, [b[2] for b in blocks], r


def edges_kernel(u_hbm, k_hbm, f_hbm, u_ref, k_ref, f_ref, out_ref, end_ref, *sems):
    pairs = ((k_hbm, k_ref), (u_hbm, u_ref), (f_hbm, f_ref))
    copies = [pltpu.make_async_copy(a, b, sem) for (a, b), sem in zip(pairs, sems)]
    for copy in copies:
        copy.start()
    lane = lax.broadcasted_iota(jnp.int32, (ROWS, NZ), 1)
    copies[0].wait()
    k = pltpu.roll(k_ref[...].reshape(ROWS, NZ), 3, 1)
    copies[1].wait()
    both = jnp.where(lane < 2, pltpu.roll(u_ref[...].reshape(ROWS, NZ), 1, 1), k)
    for i in range(ROWS // NZ):
        block = slice(i * NZ, (i + 1) * NZ)
        out_ref[:, block] = both[block].T[:8]
    index = lax.axis_index("gx")
    end_ref[...] = k_ref[jnp.where(lax.rem(index, 2) == 1, NX - 1, 0)]
    copies[2].wait()


def local_kernel(u_ref, k_ref, f_ref, rp_ref, a_ref, m_ref, inv_ref, ew_ref):
    row = lax.broadcasted_iota(jnp.int32, (NY, NZ), 0)
    lane = lax.broadcasted_iota(jnp.int32, (NY, NZ), 1)
    for x in range(NX):
        u, k = u_ref[x], k_ref[x]
        flux_y = (CY * (k + pltpu.roll(k, NY - 1, 0))) * (pltpu.roll(u, NY - 1, 0) - u)
        flux_y = jnp.where(row == NY - 1, -(CY * k) * u, flux_y)
        low_y = jnp.where(row == 0, (CY * k) * u, pltpu.roll(flux_y, 1, 0))
        flux_z = (CZ * (k + pltpu.roll(k, NZ - 1, 1))) * (pltpu.roll(u, NZ - 1, 1) - u)
        flux_z = jnp.where(lane == NZ - 1, 0.0, flux_z)
        low_z = pltpu.roll(flux_z, 1, 1)
        rp_ref[x] = u + (flux_y - low_y) + (flux_z - low_z) + 0.5 * f_ref[x]
    s = jnp.ones((NY, NZ), F32)
    e_h = s
    w = CX * (k_ref[0] + k_ref[1])
    for j in range(1, NX - 1):
        c = CX * (k_ref[j] + k_ref[j + 1])
        inv = 1.0 / (s + w + c)
        a, m = w * inv, c * inv
        inv_ref[j - 1], a_ref[j - 1], m_ref[j - 1] = inv, a, m
        e_h = e_h + a * s
        s = 1.0 + m * s
        w = m * w
    ew_ref[0], ew_ref[1], ew_ref[2] = e_h, s, w


def halo_kernel(own_ref, one_ref, two_ref, below_ref, rp_ref, a_ref, m_ref, ew_ref, k_ref, keep_ref, send_ref, rr_ref, fix_ref):
    g = lax.axis_index("gz")
    index = lax.axis_index("gx")
    core = lax.rem(index, 2)
    odd = lax.rem(g, 2) == 1
    own, one, two = own_ref[...], one_ref[...], two_ref[...]
    low = jnp.where(odd, one, two) * jnp.where(g > 0, 1.0, 0.0)
    high = jnp.where(odd, two, one) * jnp.where(g < 3, 1.0, 0.0)
    at_low = CZ * (low[2:3] + own[3:4]) * (low[0:1] - own[1:2])
    at_high = CZ * (high[3:4] + own[2:3]) * (high[1:2] - own[0:1])
    row = lax.broadcasted_iota(jnp.int32, (8, ROWS), 0)
    both = jnp.where(row == 0, at_low, jnp.where(row == 1, at_high, 0.0))
    fix_ref[...] = rows_to_lanes([(0, 0), (1, NZ - 1)], both, NZ).reshape(NX, NY, NZ)
    top = jnp.where(index == lax.axis_size("gx") - 1, CX, 0.0)
    inner = jnp.where(core == 0, NX - 1, 0)
    place = lax.rem(index, RING)
    inside = jnp.where(index >= RING, 1.0, 0.0)
    half = half_of(index)
    for which, out in ((half, keep_ref), (1 - half, send_ref)):
        ys = pl.ds(pl.multiple_of(which * HALF, HALF), HALF)
        r_h = rp_ref[0, ys] + fix_ref[0, ys]
        rr = rp_ref[1, ys] + fix_ref[1, ys]
        for j in range(1, NX - 1):
            rr_ref[j - 1, ys] = rr
            r_h = r_h + a_ref[j - 1, ys] * rr
            rr = (rp_ref[j + 1, ys] + fix_ref[j + 1, ys]) + m_ref[j - 1, ys] * rr
        out[0], out[2] = ew_ref[0, ys], ew_ref[2, ys]
        out[1] = ew_ref[1, ys] + top * k_ref[NX - 1, ys]
        out[3], out[4] = r_h, rr
        out[5] = k_ref[inner, ys]
        below, k = below_ref[ys], k_ref[0, ys]
        out[6] = jnp.where(place == 0, k, jnp.where(place == RING - 1, below * inside, CX * (below + k)))


def core_kernel(own_ref, got_ref, out_ref, parts_ref):
    index = lax.axis_index("gx")
    first = lax.rem(index, 2) == 0
    head = lax.rem(index, RING) < 2
    low = [jnp.where(first, own_ref[i], got_ref[i]) for i in range(7)]
    high = [jnp.where(first, got_ref[i], own_ref[i]) for i in range(7)]
    cut = jnp.where(head, 1.0, 0.0)
    near = jnp.where(head, 2.0 * low[2], low[2])
    e = [cut * low[0], (1.0 - cut) * low[0], low[1], high[0], high[1]]
    c = [jnp.where(head, near, low[6]), near, CX * (low[5] + high[5]), high[2]]
    r = [cut * low[3], (1.0 - cut) * low[3], low[4], high[3], high[4]]
    port, parts = reduce_chain(e, c, r)
    for i, v in enumerate(port):
        out_ref[i] = v
    out_ref[5] = jnp.where(head, low[6], high[6])
    for j, p in enumerate(parts):
        for i in range(3):
            parts_ref[3 * j + i] = p[i]


def ordered(me, refs, order, held):
    half = half_of(lax.axis_index("gx"))
    for pair, ref in zip(((0, 0),) + order, refs):
        held[jnp.bitwise_xor(me, jnp.where(half == 0, pair[0], pair[1]))] = ref[...]


def chips_kernel(own_ref, one_ref, two_ref, three_ref, after_ref, also_ref, out_ref, parts_ref, held):
    del after_ref, also_ref
    me = lax.rem(lax.axis_index("gx") // 2, 4)
    ordered(me, (own_ref, one_ref, two_ref, three_ref), X_ORDER, held)
    blocks = [[held[b, i] for i in range(5)] for b in range(4)]
    e, c, r = join(blocks)
    below = CX * (held[0, 5] + held[3, 5])
    port, parts = reduce_chain([0.0] + e, [below] + c, [0.0] + r)
    for i, v in enumerate(port):
        out_ref[i] = v
    for j, p in enumerate(parts):
        for i in range(3):
            parts_ref[3 * j + i] = p[i]


def back_kernel(own_ref, one_ref, two_ref, three_ref, chips_ref, cores_ref, after_ref, keep_ref, send_ref, held, nodes):
    del after_ref
    index = lax.axis_index("gx")
    core, x, z = lax.rem(index, 2), lax.rem(index // 2, 4), index // 8
    ordered(z, (own_ref, one_ref, two_ref, three_ref), Z_ORDER, held)
    blocks = [[held[b, i] for i in range(5)] for b in range(4)]
    e, c, r = join(blocks)
    e[1] = e[1] + c[0]
    nodes[0] = jnp.zeros((HALF, NZ), F32)
    for i, v in enumerate(solve_chain(e[1:], c[1:], r[1:])):
        nodes[i + 1] = v
    first, last = nodes[z], nodes[z + 1]
    parts = [tuple(chips_ref[3 * j + i] for i in range(3)) for j in range(4)]
    for i, v in enumerate(expand_chain(first, last, parts)):
        nodes[i] = v
    first, last = nodes[x + 1], nodes[x + 2]
    parts = [tuple(cores_ref[3 * j + i] for i in range(3)) for j in range(3)]
    v = expand_chain(first, last, parts)
    v[1] = jnp.where(x == 0, v[0], v[1])
    even = core == 0
    keep_ref[0], keep_ref[1] = jnp.where(even, v[1], v[3]), jnp.where(even, v[2], v[4])
    send_ref[0], send_ref[1] = jnp.where(even, v[3], v[1]), jnp.where(even, v[4], v[2])


def y_major(ref, x, block):
    rows = ref.reshape(ROWS, NZ)
    for t in range(NY // 8):
        rows[pl.ds(t * 8 * NX + x, 8, stride=NX), :] = block[8 * t : 8 * t + 8]


def prepare_kernel(u_ref, k_ref, a_ref, m_ref, inv_ref, rr_ref, base_ref, g_ref, h_ref, my_ref, iy_ref):
    zero = jnp.zeros((NY, NZ), F32)
    y, g, h = zero, zero, zero + 1.0
    y_major(base_ref, NX - 1, -u_ref[NX - 1])
    y_major(g_ref, NX - 1, g)
    y_major(h_ref, NX - 1, h)
    for j in range(NX - 2, 0, -1):
        m = m_ref[j - 1]
        y = rr_ref[j - 1] * inv_ref[j - 1] + m * y
        g = a_ref[j - 1] + m * g
        h = m * h
        y_major(base_ref, j, y - u_ref[j])
        y_major(g_ref, j, g)
        y_major(h_ref, j, h)
    y_major(base_ref, 0, -u_ref[0])
    y_major(g_ref, 0, zero + 1.0)
    y_major(h_ref, 0, zero)
    k2 = k_ref.reshape(ROWS, NZ)
    at = lambda y: k2[pl.ds(y, NX, stride=NY), :]
    mid = HALF
    ends = []
    for start, step in ((0, 1), (NY - 1, -1)):
        k = at(start)
        ends.append([1.0 + CY * k, k, start, step])
    while any(e[2] != mid for e in ends):
        for e in ends:
            s, k, y, step = e
            if y == mid:
                continue
            k_next = at(y + step)
            c = CY * (k + k_next)
            inv = 1.0 / (s + c)
            m = c * inv
            my_ref[y], iy_ref[y] = m, inv
            e[0] = (0.0 if y + step == mid else 1.0) + m * s
            e[1], e[2] = k_next, y + step
    iy_ref[mid] = 1.0 / (1.0 + ends[0][0] + ends[1][0])
    my_ref[mid] = jnp.zeros((NX, NZ), F32)


LEVELS = 7
STEP = 32


def z_factors(k, keep):
    lane = lax.broadcasted_iota(jnp.int32, k.shape, 1)
    up = CZ * (k + pltpu.roll(k, NZ - 1, 1))
    low = pltpu.roll(up, 1, 1)
    top = up
    e = jnp.ones(k.shape, F32)
    for n in range(LEVELS):
        s = 1 << n
        inv = 1.0 / (e + low + up)
        has_low, has_up = lane >= s + 1, lane <= NZ - 2 - s
        low_in, up_in = jnp.where(has_low, low, 0.0), jnp.where(has_up, up, 0.0)
        keep(n, low_in, up_in, inv)
        share = e * inv
        e = e + low_in * pltpu.roll(share, s, 1) + up_in * pltpu.roll(share, NZ - s, 1)
        new_low = jnp.where(has_low, low * pltpu.roll(low * inv, s, 1), low)
        up = jnp.where(has_up, up * pltpu.roll(up * inv, NZ - s, 1), up)
        low = new_low
    inv = 1.0 / (e + low + up)
    first, last = lane == 0, lane == NZ - 1
    g = jnp.where(first, 1.0, jnp.where(last, 0.0, low * inv))
    h = jnp.where(first, 0.0, jnp.where(last, 1.0, up * inv))
    inv = jnp.where(first | last, 0.0, inv)
    return g, h, jnp.where(lane == NZ - 2, top * g, 0.0), inv


def z_ports_kernel(start, k_ref, u_ref, after_ref, uy_ref, g_ref, h_ref, port_ref, f_ref, t_ref):
    del after_ref
    k2, u2 = k_ref.reshape(ROWS, NZ), u_ref.reshape(ROWS, NZ)
    for y in range(HALF):
        uy_ref[y] = u2[pl.ds(start + y, NX, stride=NY), :]
    g2, h2 = g_ref.reshape(ROWS // 2, NZ), h_ref.reshape(ROWS // 2, NZ)

    def body(i, carry):
        y = start + i * STEP
        k = jnp.concatenate([k2[pl.ds(y + n, NX, stride=NY), :] for n in range(STEP)], axis=0)
        at = pl.ds(pl.multiple_of(i * (STEP * NX), NX * STEP), NX * STEP)

        def keep(n, *values):
            for j, v in enumerate(values):
                f_ref[3 * n + j, at, :] = v

        g, h, w, inv = z_factors(k, keep)
        f_ref[3 * LEVELS, at, :] = inv
        g2[at, :], h2[at, :] = g, h
        t_ref[0, at, :], t_ref[1, at, :] = k, w
        return carry

    lax.fori_loop(0, HALF // STEP, body, 0)
    port_ref[...] = (
        lanes_to_rows([(0, None)], g2[...])
        + lanes_to_rows([(1, None)], h2[...])
        + lanes_to_rows([(2, NZ - 2)], t_ref[1])
        + lanes_to_rows([(5, 0), (6, NZ - 1)], t_ref[0])
    )[:8]


def y_kernel(keep_ref, got_ref, base_ref, gx_ref, hx_ref, my_ref, iy_ref, g0_ref, g1_ref, h0_ref, h1_ref, p0_ref, p1_ref, v_ref, out_ref, b_ref, d_ref):
    half = half_of(lax.axis_index("gx"))
    for i in range(2):
        b_ref[i, pl.ds(pl.multiple_of(half * HALF, HALF), HALF)] = keep_ref[i]
        b_ref[i, pl.ds(pl.multiple_of((1 - half) * HALF, HALF), HALF)] = got_ref[i]

    def at(y):
        first = jnp.broadcast_to(b_ref[0, y : y + 1, :], (NX, NZ))
        last = jnp.broadcast_to(b_ref[1, y : y + 1, :], (NX, NZ))
        return base_ref[y] + gx_ref[y] * first + hx_ref[y] * last

    mid = HALF
    low, high = at(0), at(NY - 1)
    for n in range(mid):
        y = n
        v_ref[y] = low * iy_ref[y]
        low = (at(y + 1) if y + 1 < mid else 0.0) + my_ref[y] * low
        y = NY - 1 - n
        if y > mid:
            v_ref[y] = high * iy_ref[y]
            high = (at(y - 1) if y - 1 > mid else 0.0) + my_ref[y] * high
    v = (at(mid) + low + high) * iy_ref[mid]
    low = high = v

    def emit(y, v):
        v_ref[y] = v
        g, h = (g0_ref, h0_ref) if y < HALF else (g1_ref, h1_ref)
        d_ref[0, y * NX : (y + 1) * NX, :] = g[y % HALF] * v
        d_ref[1, y * NX : (y + 1) * NX, :] = h[y % HALF] * v

    emit(mid, v)
    for n in range(1, mid + 1):
        y = mid - n
        low = v_ref[y] + my_ref[y] * low
        emit(y, low)
        y = mid + n
        if y < NY:
            high = v_ref[y] + my_ref[y] * high
            emit(y, high)
    out_ref[...] = (
        jnp.concatenate([p0_ref[...], p1_ref[...]], axis=1)
        + (lanes_to_rows([(3, None)], d_ref[0]) + lanes_to_rows([(4, None)], d_ref[1]))[:8]
    )


def z_local_kernel(f0_ref, f1_ref, u0_ref, u1_ref, v_ref, y_ref):
    v2, y2 = v_ref.reshape(ROWS, NZ), y_ref.reshape(ROWS, NZ)
    rows = STEP * NX

    for half, (f_ref, u_ref) in enumerate(((f0_ref, u0_ref), (f1_ref, u1_ref))):
        u2 = u_ref.reshape(ROWS // 2, NZ)

        def body(i, carry):
            at = pl.ds(pl.multiple_of(i * rows, rows), rows)
            full = pl.ds(pl.multiple_of(half * (ROWS // 2) + i * rows, rows), rows)
            r = v2[full, :]
            for n in range(LEVELS):
                s = 1 << n
                q = r * f_ref[3 * n + 2, at, :]
                r = (
                    r
                    + f_ref[3 * n, at, :] * pltpu.roll(q, s, 1)
                    + f_ref[3 * n + 1, at, :] * pltpu.roll(q, NZ - s, 1)
                )
            y2[full, :] = u2[at, :] + 2.0 * (r * f_ref[3 * LEVELS, at, :])
            return carry

        lax.fori_loop(0, HALF // STEP, body, 0)


CHUNK = 16


def final_kernel(own_ref, one_ref, two_ref, three_ref, y_ref, g0_ref, g1_ref, h0_ref, h1_ref, out_ref, held, b_ref, o_ref, *sems):
    me = lax.axis_index("gz")
    ordered(me, (own_ref, one_ref, two_ref, three_ref), L_ORDER, held)
    blocks = [[held[b, i : i + 1, :] for i in range(7)] for b in range(4)]
    e, c, r = [], [], []
    for i, b in enumerate(blocks):
        e += [b[0], b[1]]
        r += [b[3], b[4]]
        c.append(b[2])
        if i < 3:
            c.append(CZ * (b[6] + blocks[i + 1][5]))
    e[0] = e[0] + CZ * blocks[0][5]
    e[-1] = e[-1] + CZ * blocks[3][6]
    values = solve_chain(e, c, r)
    first, last = values[0], values[1]
    for b in range(1, 4):
        first = jnp.where(me == b, values[2 * b], first)
        last = jnp.where(me == b, values[2 * b + 1], last)
    row = lax.broadcasted_iota(jnp.int32, (8, ROWS), 0)
    both = jnp.where(row == 0, 2.0 * first, jnp.where(row == 1, 2.0 * last, 0.0))
    b_ref[...] = rows_to_lanes([(0, range(0, NZ)), (1, range(NZ, 2 * NZ))], both, 2 * NZ)
    o2 = o_ref.reshape(ROWS, NZ)
    copies = []
    for y in range(NY):
        ys = slice(y * NX, (y + 1) * NX)
        g, h = (g0_ref, h0_ref) if y < HALF else (g1_ref, h1_ref)
        o2[pl.ds(y, NX, stride=NY), :] = (
            y_ref[y] + g[y % HALF] * b_ref[ys, :NZ] + h[y % HALF] * b_ref[ys, NZ:]
        )
        if y % CHUNK == CHUNK - 1:
            part = pl.ds(y + 1 - CHUNK, CHUNK)
            copies.append(pltpu.make_async_copy(o_ref.at[:, part], out_ref.at[:, part], sems[y // CHUNK]))
            copies[-1].start()
    for copy in copies:
        copy.wait()


def swap(block, axis, mask):
    n = lax.axis_size(axis)
    return lax.ppermute(block, axis, [(i, i ^ mask) for i in range(n)])


def gather(block, unit, order, bits):
    got = []
    for pair in order:
        route = []
        for i in range(lax.axis_size("gx")):
            distance = pair[half_of(i)]
            route.append((i, i ^ (unit * distance) ^ flips(distance, bits)))
        got.append(lax.ppermute(block, "gx", route))
    return got


def below_target(i, n):
    place = i % RING
    if place == 0:
        return i ^ RING
    if place == RING - 1:
        return (i + RING) % n
    return i + 1 if place % 2 else i - 1


def per_device(u, k, f):
    n = lax.axis_size("gx")
    u, k, f = (pltpu.with_memory_space_constraint(t, pltpu.HBM) for t in (u, k, f))
    u, k, f, edges, end = call(
        edges_kernel,
        [(NX, NY, NZ)] * 3 + [(8, ROWS), (NY, NZ)],
        u, k, f, sems=3, ins_in=pltpu.HBM, name="edges",
    )
    nz = lax.axis_size("gz")
    inner = [
        (i * nz + j, (i ^ 1) * nz + j if j in (0, nz - 1) else i * nz + (j ^ 3))
        for i in range(n)
        for j in range(nz)
    ]
    one, two = swap(edges, "gz", 1), lax.ppermute(edges, ("gx", "gz"), inner)
    below = lax.ppermute(end, "gx", [(i, below_target(i, n)) for i in range(n)])
    rp, a, m, inv, ew = call(
        local_kernel,
        [(NX, NY, NZ), (NX - 2, NY, NZ), (NX - 2, NY, NZ), (NX - 2, NY, NZ), (3, NY, NZ)],
        u, k, f, name="local",
    )
    keep, send, rr = call(
        halo_kernel,
        [(7, HALF, NZ), (7, HALF, NZ), (NX - 2, NY, NZ)],
        edges, one, two, below, rp, a, m, ew, k, scratch=[(NX, NY, NZ)], name="halo",
    )
    got = swap(send, "gx", 1)
    chip, core_parts = call(core_kernel, [(6, HALF, NZ), (9, HALF, NZ)], keep, got, name="core")
    x_got = gather(chip, 2, X_ORDER, X_FLIP)
    base, gx, hx, my, iy = call(
        prepare_kernel, [(NY, NX, NZ)] * 5, u, k, a, m, inv, rr, name="prepare"
    )
    z_shapes = [(HALF, NX, NZ)] * 3 + [(8, ROWS // 2), (3 * LEVELS + 1, ROWS // 2, NZ)]
    u0, g0, h0, p0, f0 = call(
        functools.partial(z_ports_kernel, 0),
        z_shapes, k, u, chip, scratch=[(2, ROWS // 2, NZ)], name="z_ports",
    )
    group, chip_parts = call(
        chips_kernel,
        [(5, HALF, NZ), (12, HALF, NZ)],
        chip, *x_got, my, p0, scratch=[(4, 6, HALF, NZ)], name="chips",
    )
    z_got = gather(group, 8, Z_ORDER, Z_FLIP)
    u1, g1, h1, p1, f1 = call(
        functools.partial(z_ports_kernel, HALF),
        z_shapes, k, u, group, scratch=[(2, ROWS // 2, NZ)], name="z_ports",
    )
    keep, send = call(
        back_kernel,
        [(2, HALF, NZ), (2, HALF, NZ)],
        group, *z_got, chip_parts, core_parts, p1,
        scratch=[(4, 5, HALF, NZ), (6, HALF, NZ)], name="back",
    )
    got = swap(send, "gx", 1)
    v, message = call(
        y_kernel,
        [(NY, NX, NZ), (8, ROWS)],
        keep, got, base, gx, hx, my, iy, g0, g1, h0, h1, p0, p1,
        scratch=[(2, NY, NZ), (2, ROWS, NZ)], name="y_solve",
    )
    l_got = [swap(message, "gz", i) for i, _ in L_ORDER]
    yz, = call(z_local_kernel, [(NY, NX, NZ)], f0, f1, u0, u1, v, name="z_local")
    out, = call(
        final_kernel,
        [(NX, NY, NZ)],
        message, *l_got, yz, g0, g1, h0, h1,
        scratch=[(4, 8, ROWS), (ROWS, 2 * NZ), (NX, NY, NZ)], sems=NY // CHUNK,
        outs_in=pltpu.HBM, name="final",
    )
    return out


def solution(mesh):
    spec = P("gx", None, "gz")
    return jax.shard_map(
        per_device, mesh=mesh, in_specs=(spec, spec, spec), out_specs=spec, check_vma=False
    )
```

```python
import functools

import jax
import jax.numpy as jnp
from jax import lax
from jax.experimental import pallas as pl
from jax.experimental.pallas import tpu as pltpu
from jax.sharding import PartitionSpec as P

NX, NY, NZ = 8, 64, 128
ROWS = NX * NY
HALF = NY // 2
RING = 8
CX = 0.25 * 16.0 * NX * NX
CY = 0.25 * 2.0
CZ = 0.25 * 0.5 * NZ * NZ
F32 = jnp.float32
VMEM_LIMIT = 24 * 1024 * 1024
BF16 = jnp.bfloat16
X_ORDER, Z_ORDER, L_ORDER = ((3, 2), (2, 3), (1, 1)), ((3, 2), (2, 3), (1, 1)), ((3, 3), (2, 2), (1, 1))
X_FLIP, Z_FLIP = 2, 2


def flips(distance, bits):
    both = distance & bits
    return (both ^ (both >> 1)) & 1


def half_of(index):
    return (index & 1) ^ flips((index >> 1) & 3, X_FLIP) ^ flips(index >> 3, Z_FLIP)


def call(kernel, outs, *args, scratch=(), sems=0, ins_in=pltpu.VMEM, outs_in=pltpu.VMEM, flops=0, name=None):
    shapes = [jax.ShapeDtypeStruct(s, F32) for s in outs]
    nbytes = sum(4 * a.size for a in args) + sum(4 * s.size for s in shapes)
    return pl.pallas_call(
        kernel,
        out_shape=shapes,
        in_specs=[pl.BlockSpec(memory_space=ins_in) for _ in args],
        out_specs=[pl.BlockSpec(memory_space=outs_in) for _ in outs],
        scratch_shapes=[pltpu.VMEM(s, F32) for s in scratch]
        + [pltpu.SemaphoreType.DMA] * sems,
        compiler_params=pltpu.CompilerParams(vmem_limit_bytes=VMEM_LIMIT),
        cost_estimate=pl.CostEstimate(flops=flops, bytes_accessed=nbytes, transcendentals=0),
        name=name,
    )(*args)


def pieces(x):
    high = x.astype(BF16).astype(F32)
    rest = x - high
    middle = rest.astype(BF16).astype(F32)
    return high, middle, rest - middle


def lanes_to_rows(entries, block):
    high, middle, low = (p.astype(BF16) for p in pieces(block))
    select = selector(entries, 16, NZ).astype(BF16)
    dims = (((1,), (1,)), ((), ()))
    return lax.dot_general(
        jnp.concatenate([select, select], axis=1),
        jnp.concatenate([high, middle], axis=1),
        dims,
        preferred_element_type=F32,
    ) + lax.dot_general(select, low, dims, preferred_element_type=F32)


def rows_to_lanes(entries, rows, lanes):
    both = jnp.concatenate(pieces(rows) + (jnp.zeros_like(rows),), axis=0).astype(BF16)
    select = selector([(r + 8 * i, l) for i in range(3) for r, l in entries], 32, lanes)
    return lax.dot_general(
        both, select.astype(BF16), (((0,), (0,)), ((), ())), preferred_element_type=F32
    )


def selector(entries, rows, lanes):
    row = lax.broadcasted_iota(jnp.int32, (rows, lanes), 0)
    lane = lax.broadcasted_iota(jnp.int32, (rows, lanes), 1)
    hit = None
    for r, l in entries:
        one = row == r
        if isinstance(l, range):
            one = one & (lane >= l.start) & (lane < l.stop)
        elif l is not None:
            one = one & (lane == l)
        hit = one if hit is None else (hit | one)
    return jnp.where(hit, 1.0, 0.0).astype(F32)


def reduce_chain(e, c, r):
    n = len(e)
    e_h, r_h = e[0], r[0]
    s, w, rr = e[1], c[0], r[1]
    parts = []
    for j in range(1, n - 1):
        inv = 1.0 / (s + w + c[j])
        a, m = w * inv, c[j] * inv
        parts.append((a, m, rr * inv))
        e_h = e_h + a * s
        r_h = r_h + a * rr
        s = e[j + 1] + m * s
        rr = r[j + 1] + m * rr
        w = m * w
    return (e_h, s, w, r_h, rr), parts


def expand_chain(first, last, parts):
    values = [last]
    for a, m, q in reversed(parts):
        values.append(q + a * first + m * values[-1])
    values.append(first)
    return values[::-1]


def solve_chain(e, c, r):
    n = len(e)
    mid = n // 2
    low, high = [], []
    s, rr = e[0], r[0]
    t, tt = e[n - 1], r[n - 1]
    for j in range(mid):
        inv = 1.0 / (s + c[j])
        m = c[j] * inv
        low.append((m, rr * inv))
        s, rr = e[j + 1] + m * s, r[j + 1] + m * rr
        i = n - 1 - j
        if i > mid:
            inv = 1.0 / (t + c[i - 1])
            m = c[i - 1] * inv
            high.append((m, tt * inv))
            t, tt = m * t, m * tt
            if i - 1 > mid:
                t, tt = e[i - 1] + t, r[i - 1] + tt
    values = [None] * n
    values[mid] = (rr + tt) / (s + t)
    for j in range(mid - 1, -1, -1):
        m, q = low[j]
        values[j] = q + m * values[j + 1]
    for i in range(mid + 1, n):
        m, q = high[n - 1 - i]
        values[i] = q + m * values[i - 1]
    return values


def join(blocks):
    e = [blocks[0][0]]
    r = [blocks[0][3]]
    for i, b in enumerate(blocks):
        e.append(b[1] + blocks[i + 1][0] if i + 1 < len(blocks) else b[1])
        r.append(b[4] + blocks[i + 1][3] if i + 1 < len(blocks) else b[4])
    return e, [b[2] for b in blocks], r


def edges_kernel(u_hbm, k_hbm, f_hbm, u_ref, k_ref, f_ref, out_ref, end_ref, *sems):
    pairs = ((k_hbm, k_ref), (u_hbm, u_ref), (f_hbm, f_ref))
    copies = [pltpu.make_async_copy(a, b, sem) for (a, b), sem in zip(pairs, sems)]
    for copy in copies:
        copy.start()
    lane = lax.broadcasted_iota(jnp.int32, (ROWS, NZ), 1)
    copies[0].wait()
    k = pltpu.roll(k_ref[...].reshape(ROWS, NZ), 3, 1)
    copies[1].wait()
    both = jnp.where(lane < 2, pltpu.roll(u_ref[...].reshape(ROWS, NZ), 1, 1), k)
    for i in range(ROWS // NZ):
        block = slice(i * NZ, (i + 1) * NZ)
        out_ref[:, block] = both[block].T[:8]
    index = lax.axis_index("gx")
    end_ref[...] = k_ref[jnp.where(lax.rem(index, 2) == 1, NX - 1, 0)]
    copies[2].wait()


def local_kernel(u_ref, k_ref, f_ref, rp_ref, a_ref, m_ref, inv_ref, ew_ref):
    row = lax.broadcasted_iota(jnp.int32, (NY, NZ), 0)
    lane = lax.broadcasted_iota(jnp.int32, (NY, NZ), 1)
    for x in range(NX):
        u, k = u_ref[x], k_ref[x]
        flux_y = (CY * (k + pltpu.roll(k, NY - 1, 0))) * (pltpu.roll(u, NY - 1, 0) - u)
        flux_y = jnp.where(row == NY - 1, -(CY * k) * u, flux_y)
        low_y = jnp.where(row == 0, (CY * k) * u, pltpu.roll(flux_y, 1, 0))
        flux_z = (CZ * (k + pltpu.roll(k, NZ - 1, 1))) * (pltpu.roll(u, NZ - 1, 1) - u)
        flux_z = jnp.where(lane == NZ - 1, 0.0, flux_z)
        low_z = pltpu.roll(flux_z, 1, 1)
        rp_ref[x] = u + (flux_y - low_y) + (flux_z - low_z) + 0.5 * f_ref[x]
    s = jnp.ones((NY, NZ), F32)
    e_h = s
    w = CX * (k_ref[0] + k_ref[1])
    for j in range(1, NX - 1):
        c = CX * (k_ref[j] + k_ref[j + 1])
        inv = 1.0 / (s + w + c)
        a, m = w * inv, c * inv
        inv_ref[j - 1], a_ref[j - 1], m_ref[j - 1] = inv, a, m
        e_h = e_h + a * s
        s = 1.0 + m * s
        w = m * w
    ew_ref[0], ew_ref[1], ew_ref[2] = e_h, s, w


def halo_kernel(own_ref, one_ref, two_ref, below_ref, rp_ref, a_ref, m_ref, ew_ref, k_ref, keep_ref, send_ref, rr_ref, fix_ref):
    g = lax.axis_index("gz")
    index = lax.axis_index("gx")
    core = lax.rem(index, 2)
    odd = lax.rem(g, 2) == 1
    own, one, two = own_ref[...], one_ref[...], two_ref[...]
    low = jnp.where(odd, one, two) * jnp.where(g > 0, 1.0, 0.0)
    high = jnp.where(odd, two, one) * jnp.where(g < 3, 1.0, 0.0)
    at_low = CZ * (low[2:3] + own[3:4]) * (low[0:1] - own[1:2])
    at_high = CZ * (high[3:4] + own[2:3]) * (high[1:2] - own[0:1])
    row = lax.broadcasted_iota(jnp.int32, (8, ROWS), 0)
    both = jnp.where(row == 0, at_low, jnp.where(row == 1, at_high, 0.0))
    fix_ref[...] = rows_to_lanes([(0, 0), (1, NZ - 1)], both, NZ).reshape(NX, NY, NZ)
    top = jnp.where(index == lax.axis_size("gx") - 1, CX, 0.0)
    inner = jnp.where(core == 0, NX - 1, 0)
    place = lax.rem(index, RING)
    inside = jnp.where(index >= RING, 1.0, 0.0)
    half = half_of(index)
    for which, out in ((half, keep_ref), (1 - half, send_ref)):
        ys = pl.ds(pl.multiple_of(which * HALF, HALF), HALF)
        r_h = rp_ref[0, ys] + fix_ref[0, ys]
        rr = rp_ref[1, ys] + fix_ref[1, ys]
        for j in range(1, NX - 1):
            rr_ref[j - 1, ys] = rr
            r_h = r_h + a_ref[j - 1, ys] * rr
            rr = (rp_ref[j + 1, ys] + fix_ref[j + 1, ys]) + m_ref[j - 1, ys] * rr
        out[0], out[2] = ew_ref[0, ys], ew_ref[2, ys]
        out[1] = ew_ref[1, ys] + top * k_ref[NX - 1, ys]
        out[3], out[4] = r_h, rr
        out[5] = k_ref[inner, ys]
        below, k = below_ref[ys], k_ref[0, ys]
        out[6] = jnp.where(place == 0, k, jnp.where(place == RING - 1, below * inside, CX * (below + k)))


def core_kernel(own_ref, got_ref, out_ref, parts_ref):
    index = lax.axis_index("gx")
    first = lax.rem(index, 2) == 0
    head = lax.rem(index, RING) < 2
    low = [jnp.where(first, own_ref[i], got_ref[i]) for i in range(7)]
    high = [jnp.where(first, got_ref[i], own_ref[i]) for i in range(7)]
    cut = jnp.where(head, 1.0, 0.0)
    near = jnp.where(head, 2.0 * low[2], low[2])
    e = [cut * low[0], (1.0 - cut) * low[0], low[1], high[0], high[1]]
    c = [jnp.where(head, near, low[6]), near, CX * (low[5] + high[5]), high[2]]
    r = [cut * low[3], (1.0 - cut) * low[3], low[4], high[3], high[4]]
    port, parts = reduce_chain(e, c, r)
    for i, v in enumerate(port):
        out_ref[i] = v
    out_ref[5] = jnp.where(head, low[6], high[6])
    for j, p in enumerate(parts):
        for i in range(3):
            parts_ref[3 * j + i] = p[i]


def ordered(me, refs, order, held):
    half = half_of(lax.axis_index("gx"))
    for pair, ref in zip(((0, 0),) + order, refs):
        held[jnp.bitwise_xor(me, jnp.where(half == 0, pair[0], pair[1]))] = ref[...]


def chips_kernel(own_ref, one_ref, two_ref, three_ref, after_ref, also_ref, out_ref, parts_ref, held):
    del after_ref, also_ref
    me = lax.rem(lax.axis_index("gx") // 2, 4)
    ordered(me, (own_ref, one_ref, two_ref, three_ref), X_ORDER, held)
    blocks = [[held[b, i] for i in range(5)] for b in range(4)]
    e, c, r = join(blocks)
    below = CX * (held[0, 5] + held[3, 5])
    port, parts = reduce_chain([0.0] + e, [below] + c, [0.0] + r)
    for i, v in enumerate(port):
        out_ref[i] = v
    for j, p in enumerate(parts):
        for i in range(3):
            parts_ref[3 * j + i] = p[i]


def back_kernel(own_ref, one_ref, two_ref, three_ref, chips_ref, cores_ref, after_ref, keep_ref, send_ref, held, nodes):
    del after_ref
    index = lax.axis_index("gx")
    core, x, z = lax.rem(index, 2), lax.rem(index // 2, 4), index // 8
    ordered(z, (own_ref, one_ref, two_ref, three_ref), Z_ORDER, held)
    blocks = [[held[b, i] for i in range(5)] for b in range(4)]
    e, c, r = join(blocks)
    e[1] = e[1] + c[0]
    nodes[0] = jnp.zeros((HALF, NZ), F32)
    for i, v in enumerate(solve_chain(e[1:], c[1:], r[1:])):
        nodes[i + 1] = v
    first, last = nodes[z], nodes[z + 1]
    parts = [tuple(chips_ref[3 * j + i] for i in range(3)) for j in range(4)]
    for i, v in enumerate(expand_chain(first, last, parts)):
        nodes[i] = v
    first, last = nodes[x + 1], nodes[x + 2]
    parts = [tuple(cores_ref[3 * j + i] for i in range(3)) for j in range(3)]
    v = expand_chain(first, last, parts)
    v[1] = jnp.where(x == 0, v[0], v[1])
    even = core == 0
    keep_ref[0], keep_ref[1] = jnp.where(even, v[1], v[3]), jnp.where(even, v[2], v[4])
    send_ref[0], send_ref[1] = jnp.where(even, v[3], v[1]), jnp.where(even, v[4], v[2])


def y_major(ref, x, block):
    rows = ref.reshape(ROWS, NZ)
    for t in range(NY // 8):
        rows[pl.ds(t * 8 * NX + x, 8, stride=NX), :] = block[8 * t : 8 * t + 8]


def prepare_kernel(u_ref, k_ref, a_ref, m_ref, inv_ref, rr_ref, base_ref, g_ref, h_ref, my_ref, iy_ref):
    zero = jnp.zeros((NY, NZ), F32)
    y, g, h = zero, zero, zero + 1.0
    y_major(base_ref, NX - 1, -u_ref[NX - 1])
    y_major(g_ref, NX - 1, g)
    y_major(h_ref, NX - 1, h)
    for j in range(NX - 2, 0, -1):
        m = m_ref[j - 1]
        y = rr_ref[j - 1] * inv_ref[j - 1] + m * y
        g = a_ref[j - 1] + m * g
        h = m * h
        y_major(base_ref, j, y - u_ref[j])
        y_major(g_ref, j, g)
        y_major(h_ref, j, h)
    y_major(base_ref, 0, -u_ref[0])
    y_major(g_ref, 0, zero + 1.0)
    y_major(h_ref, 0, zero)
    k2 = k_ref.reshape(ROWS, NZ)
    at = lambda y: k2[pl.ds(y, NX, stride=NY), :]
    mid = HALF
    ends = []
    for start, step in ((0, 1), (NY - 1, -1)):
        k = at(start)
        ends.append([1.0 + CY * k, k, start, step])
    while any(e[2] != mid for e in ends):
        for e in ends:
            s, k, y, step = e
            if y == mid:
                continue
            k_next = at(y + step)
            c = CY * (k + k_next)
            inv = 1.0 / (s + c)
            m = c * inv
            my_ref[y], iy_ref[y] = m, inv
            e[0] = (0.0 if y + step == mid else 1.0) + m * s
            e[1], e[2] = k_next, y + step
    iy_ref[mid] = 1.0 / (1.0 + ends[0][0] + ends[1][0])
    my_ref[mid] = jnp.zeros((NX, NZ), F32)


LEVELS = 7
STEP = 32


def z_factors(k, keep):
    lane = lax.broadcasted_iota(jnp.int32, k.shape, 1)
    up = CZ * (k + pltpu.roll(k, NZ - 1, 1))
    low = pltpu.roll(up, 1, 1)
    top = up
    e = jnp.ones(k.shape, F32)
    for n in range(LEVELS):
        s = 1 << n
        inv = 1.0 / (e + low + up)
        has_low, has_up = lane >= s + 1, lane <= NZ - 2 - s
        low_in, up_in = jnp.where(has_low, low, 0.0), jnp.where(has_up, up, 0.0)
        keep(n, low_in, up_in, inv)
        share = e * inv
        e = e + low_in * pltpu.roll(share, s, 1) + up_in * pltpu.roll(share, NZ - s, 1)
        new_low = jnp.where(has_low, low * pltpu.roll(low * inv, s, 1), low)
        up = jnp.where(has_up, up * pltpu.roll(up * inv, NZ - s, 1), up)
        low = new_low
    inv = 1.0 / (e + low + up)
    first, last = lane == 0, lane == NZ - 1
    g = jnp.where(first, 1.0, jnp.where(last, 0.0, low * inv))
    h = jnp.where(first, 0.0, jnp.where(last, 1.0, up * inv))
    inv = jnp.where(first | last, 0.0, inv)
    return g, h, jnp.where(lane == NZ - 2, top * g, 0.0), inv


def z_ports_kernel(start, k_ref, u_ref, after_ref, uy_ref, g_ref, h_ref, port_ref, f_ref, t_ref):
    del after_ref
    k2, u2 = k_ref.reshape(ROWS, NZ), u_ref.reshape(ROWS, NZ)
    for y in range(HALF):
        uy_ref[y] = u2[pl.ds(start + y, NX, stride=NY), :]
    g2, h2 = g_ref.reshape(ROWS // 2, NZ), h_ref.reshape(ROWS // 2, NZ)

    def body(i, carry):
        y = start + i * STEP
        k = jnp.concatenate([k2[pl.ds(y + n, NX, stride=NY), :] for n in range(STEP)], axis=0)
        at = pl.ds(pl.multiple_of(i * (STEP * NX), NX * STEP), NX * STEP)

        def keep(n, *values):
            for j, v in enumerate(values):
                f_ref[3 * n + j, at, :] = v

        g, h, w, inv = z_factors(k, keep)
        f_ref[3 * LEVELS, at, :] = inv
        g2[at, :], h2[at, :] = g, h
        t_ref[0, at, :], t_ref[1, at, :] = k, w
        return carry

    lax.fori_loop(0, HALF // STEP, body, 0)
    port_ref[...] = (
        lanes_to_rows([(0, None)], g2[...])
        + lanes_to_rows([(1, None)], h2[...])
        + lanes_to_rows([(2, NZ - 2)], t_ref[1])
        + lanes_to_rows([(5, 0), (6, NZ - 1)], t_ref[0])
    )[:8]


def y_kernel(keep_ref, got_ref, base_ref, gx_ref, hx_ref, my_ref, iy_ref, g0_ref, g1_ref, h0_ref, h1_ref, p0_ref, p1_ref, v_ref, out_ref, b_ref, d_ref):
    half = half_of(lax.axis_index("gx"))
    for i in range(2):
        b_ref[i, pl.ds(pl.multiple_of(half * HALF, HALF), HALF)] = keep_ref[i]
        b_ref[i, pl.ds(pl.multiple_of((1 - half) * HALF, HALF), HALF)] = got_ref[i]

    def at(y):
        first = jnp.broadcast_to(b_ref[0, y : y + 1, :], (NX, NZ))
        last = jnp.broadcast_to(b_ref[1, y : y + 1, :], (NX, NZ))
        return base_ref[y] + gx_ref[y] * first + hx_ref[y] * last

    mid = HALF
    low, high = at(0), at(NY - 1)
    for n in range(mid):
        y = n
        v_ref[y] = low * iy_ref[y]
        low = (at(y + 1) if y + 1 < mid else 0.0) + my_ref[y] * low
        y = NY - 1 - n
        if y > mid:
            v_ref[y] = high * iy_ref[y]
            high = (at(y - 1) if y - 1 > mid else 0.0) + my_ref[y] * high
    v = (at(mid) + low + high) * iy_ref[mid]
    low = high = v

    def emit(y, v):
        v_ref[y] = v
        g, h = (g0_ref, h0_ref) if y < HALF else (g1_ref, h1_ref)
        d_ref[0, y * NX : (y + 1) * NX, :] = g[y % HALF] * v
        d_ref[1, y * NX : (y + 1) * NX, :] = h[y % HALF] * v

    emit(mid, v)
    for n in range(1, mid + 1):
        y = mid - n
        low = v_ref[y] + my_ref[y] * low
        emit(y, low)
        y = mid + n
        if y < NY:
            high = v_ref[y] + my_ref[y] * high
            emit(y, high)
    out_ref[...] = (
        jnp.concatenate([p0_ref[...], p1_ref[...]], axis=1)
        + (lanes_to_rows([(3, None)], d_ref[0]) + lanes_to_rows([(4, None)], d_ref[1]))[:8]
    )


def z_local_kernel(f0_ref, f1_ref, u0_ref, u1_ref, v_ref, y_ref):
    v2, y2 = v_ref.reshape(ROWS, NZ), y_ref.reshape(ROWS, NZ)
    rows = STEP * NX

    for half, (f_ref, u_ref) in enumerate(((f0_ref, u0_ref), (f1_ref, u1_ref))):
        u2 = u_ref.reshape(ROWS // 2, NZ)

        def body(i, carry):
            at = pl.ds(pl.multiple_of(i * rows, rows), rows)
            full = pl.ds(pl.multiple_of(half * (ROWS // 2) + i * rows, rows), rows)
            r = v2[full, :]
            for n in range(LEVELS):
                s = 1 << n
                q = r * f_ref[3 * n + 2, at, :]
                r = (
                    r
                    + f_ref[3 * n, at, :] * pltpu.roll(q, s, 1)
                    + f_ref[3 * n + 1, at, :] * pltpu.roll(q, NZ - s, 1)
                )
            y2[full, :] = u2[at, :] + 2.0 * (r * f_ref[3 * LEVELS, at, :])
            return carry

        lax.fori_loop(0, HALF // STEP, body, 0)


CHUNK = 16


def final_kernel(own_ref, one_ref, two_ref, three_ref, y_ref, g0_ref, g1_ref, h0_ref, h1_ref, out_ref, held, b_ref, o_ref, *sems):
    me = lax.axis_index("gz")
    ordered(me, (own_ref, one_ref, two_ref, three_ref), L_ORDER, held)
    blocks = [[held[b, i : i + 1, :] for i in range(7)] for b in range(4)]
    e, c, r = [], [], []
    for i, b in enumerate(blocks):
        e += [b[0], b[1]]
        r += [b[3], b[4]]
        c.append(b[2])
        if i < 3:
            c.append(CZ * (b[6] + blocks[i + 1][5]))
    e[0] = e[0] + CZ * blocks[0][5]
    e[-1] = e[-1] + CZ * blocks[3][6]
    values = solve_chain(e, c, r)
    first, last = values[0], values[1]
    for b in range(1, 4):
        first = jnp.where(me == b, values[2 * b], first)
        last = jnp.where(me == b, values[2 * b + 1], last)
    row = lax.broadcasted_iota(jnp.int32, (8, ROWS), 0)
    both = jnp.where(row == 0, 2.0 * first, jnp.where(row == 1, 2.0 * last, 0.0))
    b_ref[...] = rows_to_lanes([(0, range(0, NZ)), (1, range(NZ, 2 * NZ))], both, 2 * NZ)
    o2 = o_ref.reshape(ROWS, NZ)
    copies = []
    for y in range(NY):
        ys = slice(y * NX, (y + 1) * NX)
        g, h = (g0_ref, h0_ref) if y < HALF else (g1_ref, h1_ref)
        o2[pl.ds(y, NX, stride=NY), :] = (
            y_ref[y] + g[y % HALF] * b_ref[ys, :NZ] + h[y % HALF] * b_ref[ys, NZ:]
        )
        if y % CHUNK == CHUNK - 1:
            part = pl.ds(y + 1 - CHUNK, CHUNK)
            copies.append(pltpu.make_async_copy(o_ref.at[:, part], out_ref.at[:, part], sems[y // CHUNK]))
            copies[-1].start()
    for copy in copies:
        copy.wait()


def swap(block, axis, mask):
    n = lax.axis_size(axis)
    return lax.ppermute(block, axis, [(i, i ^ mask) for i in range(n)])


def gather(block, unit, order, bits):
    got = []
    for pair in order:
        route = []
        for i in range(lax.axis_size("gx")):
            distance = pair[half_of(i)]
            route.append((i, i ^ (unit * distance) ^ flips(distance, bits)))
        got.append(lax.ppermute(block, "gx", route))
    return got


def below_target(i, n):
    place = i % RING
    if place == 0:
        return i ^ RING
    if place == RING - 1:
        return (i + RING) % n
    return i + 1 if place % 2 else i - 1


def per_device(u, k, f):
    n = lax.axis_size("gx")
    u, k, f = (pltpu.with_memory_space_constraint(t, pltpu.HBM) for t in (u, k, f))
    u, k, f, edges, end = call(
        edges_kernel,
        [(NX, NY, NZ)] * 3 + [(8, ROWS), (NY, NZ)],
        u, k, f, sems=3, ins_in=pltpu.HBM, name="edges",
    )
    nz = lax.axis_size("gz")
    inner = [
        (i * nz + j, (i ^ 1) * nz + j if j in (0, nz - 1) else i * nz + (j ^ 3))
        for i in range(n)
        for j in range(nz)
    ]
    one, two = swap(edges, "gz", 1), lax.ppermute(edges, ("gx", "gz"), inner)
    below = lax.ppermute(end, "gx", [(i, below_target(i, n)) for i in range(n)])
    rp, a, m, inv, ew = call(
        local_kernel,
        [(NX, NY, NZ), (NX - 2, NY, NZ), (NX - 2, NY, NZ), (NX - 2, NY, NZ), (3, NY, NZ)],
        u, k, f, name="local",
    )
    keep, send, rr = call(
        halo_kernel,
        [(7, HALF, NZ), (7, HALF, NZ), (NX - 2, NY, NZ)],
        edges, one, two, below, rp, a, m, ew, k, scratch=[(NX, NY, NZ)], name="halo",
    )
    got = swap(send, "gx", 1)
    chip, core_parts = call(core_kernel, [(6, HALF, NZ), (9, HALF, NZ)], keep, got, name="core")
    x_got = gather(chip, 2, X_ORDER, X_FLIP)
    base, gx, hx, my, iy = call(
        prepare_kernel, [(NY, NX, NZ)] * 5, u, k, a, m, inv, rr, name="prepare"
    )
    z_shapes = [(HALF, NX, NZ)] * 3 + [(8, ROWS // 2), (3 * LEVELS + 1, ROWS // 2, NZ)]
    u0, g0, h0, p0, f0 = call(
        functools.partial(z_ports_kernel, 0),
        z_shapes, k, u, chip, scratch=[(2, ROWS // 2, NZ)], name="z_ports",
    )
    group, chip_parts = call(
        chips_kernel,
        [(5, HALF, NZ), (12, HALF, NZ)],
        chip, *x_got, my, p0, scratch=[(4, 6, HALF, NZ)], name="chips",
    )
    z_got = gather(group, 8, Z_ORDER, Z_FLIP)
    u1, g1, h1, p1, f1 = call(
        functools.partial(z_ports_kernel, HALF),
        z_shapes, k, u, group, scratch=[(2, ROWS // 2, NZ)], name="z_ports",
    )
    keep, send = call(
        back_kernel,
        [(2, HALF, NZ), (2, HALF, NZ)],
        group, *z_got, chip_parts, core_parts, p1,
        scratch=[(4, 5, HALF, NZ), (6, HALF, NZ)], name="back",
    )
    got = swap(send, "gx", 1)
    v, message = call(
        y_kernel,
        [(NY, NX, NZ), (8, ROWS)],
        keep, got, base, gx, hx, my, iy, g0, g1, h0, h1, p0, p1,
        scratch=[(2, NY, NZ), (2, ROWS, NZ)], name="y_solve",
    )
    l_got = [swap(message, "gz", i) for i, _ in L_ORDER]
    yz, = call(z_local_kernel, [(NY, NX, NZ)], f0, f1, u0, u1, v, name="z_local")
    out, = call(
        final_kernel,
        [(NX, NY, NZ)],
        message, *l_got, yz, g0, g1, h0, h1,
        scratch=[(4, 8, ROWS), (ROWS, 2 * NZ), (NX, NY, NZ)], sems=NY // CHUNK,
        outs_in=pltpu.HBM, name="final",
    )
    return out


def solution(mesh):
    spec = P("gx", None, "gz")
    return jax.shard_map(
        per_device, mesh=mesh, in_specs=(spec, spec, spec), out_specs=spec, check_vma=False
    )
```
